32 devices in a mesh: req: 4 (over y, x), tile: 8 (over z, core).
Axes of the slice: x: 2, y: 2, z: 4, core: 2. Of those that a mesh axis runs over, the one named last changes fastest.
Arguments:
- image: bfloat16 [8, 4096, 2432], P('req', 'tile'), may hold values from -40 to 40
- text: bfloat16 [8, 154, 2432], P('req'), may hold values from -40 to 40
- pooled: float32 [8, 2432], P('req'), may hold values from -6 to 6
- timesteps: int32 [8], P('req'), may hold values from 0 to 999
- lengths: int32 [8], P('req'), may hold values from 1 to 4096, 16384 in all
- w_time: bfloat16 [256, 2432], replicated, may hold values from -0.375 to 0.375
- w_mod: bfloat16 [2432, 9728], P(None, 'tile'), may hold values from -0.125 to 0.125
- w_img: bfloat16 [2432, 6144], P(None, ('req', 'tile')), may hold values from -0.125 to 0.125
- w_txt: bfloat16 [2432, 6144], P(None, 'tile'), may hold values from -0.125 to 0.125
- q_gain: float32 [64], replicated, may hold values from 1 to 2.5
- k_gain: float32 [64], replicated, may hold values from 1 to 2.5
- text_q_gain: float32 [64], replicated, may hold values from 1 to 2.5
- text_k_gain: float32 [64], replicated, may hold values from 1 to 2.5
Outputs:
- image_attention: bfloat16 [8, 4096, 2048], P('req', 'tile')
- text_attention: bfloat16 [8, 154, 2048], P('req', None, 'tile')
The draws below stay inside these ranges and needn't reach their ends.
Inputs may be any that keep to these rules, and one draw needn't show every extreme that they name: `lengths`: the image token counts of all 8 requests sum to 16384, and the largest is exactly 4096.
All inputs are finite; a program needn't handle non-finite values. No bound on the sum of `lengths` on one device may be relied on, other than what follows from the above.
Results may differ from the reference program's by a relative error of at most 0.02.
Values may be sent and summed in bfloat16 or wider, within the bound.
No kernel may reach another device: no remote copies, remote signals or barrier semaphores. Data moves between devices by JAX's collectives and lax.ppermute only.
A program may use at most 192 MiB of HBM per device.

```python
import math
import jax
import jax.numpy as jnp
import numpy as np
from jax import lax

D = 2432
HEADS = 32
HD = 64
FREQ = 256
TXT = 154
LMAX = 4096
REQS = 8
TOTAL = 16384


def scaled_field(key, shape):
    first, second, third = jax.random.split(key, 3)
    row_scale = jnp.exp(jax.random.uniform(second, shape[:-1] + (1,), jnp.float32, 0.0, math.log(10.0)))
    column_scale = jnp.exp(jax.random.uniform(third, (shape[-1],), jnp.float32, 0.0, math.log(10.0)))
    noise = jax.random.truncated_normal(first, -4.0, 4.0, shape, jnp.float32)
    return (noise * row_scale * column_scale * 0.1).astype(jnp.bfloat16)


def draw_image(key, part):
    return scaled_field(jax.random.fold_in(key, 11), (REQS, LMAX, D))


def draw_text(key, part):
    return scaled_field(jax.random.fold_in(key, 12), (REQS, TXT, D))


def place_ends(result, own_key, smallest, largest):
    longest = result.shape.index(max(result.shape))
    spots = []
    for shift in (0, 1):
        where = [jax.random.randint(jax.random.fold_in(own_key, axis), (), 0, length) for axis, length in enumerate(result.shape)]
        where[longest] = (where[longest] + shift) % result.shape[longest]
        spots.append(tuple(where))
    return result.at[spots[0]].set(smallest).at[spots[1]].set(largest)


def steps_of(rng, dims, cuts, smallest, high):
    def one(axis_at, blocks):
        steps = jax.random.uniform(jax.random.fold_in(jax.random.fold_in(rng, 6), axis_at), (blocks,), jnp.float32, smallest / len(cuts), high / len(cuts))
        return jnp.repeat(jnp.exp(steps), dims[axis_at] // blocks).reshape((-1,) + (1,) * (len(dims) - axis_at - 1))

    level = one(*cuts[0])
    for cut in cuts[1:]:
        level = level * one(*cut)
    return level


def profile(number_of, total, limit, skew):
    loads = [(1 << 20) // math.isqrt(grade ** skew) + 1 for grade in range(2, number_of + 1)]
    surplus, counts = total - limit - (number_of - 1), [1] * (number_of - 1)
    while surplus > 0:
        candidates = [i for i in range(number_of - 1) if counts[i] < limit]
        whole, left = sum([loads[i] for i in candidates]), surplus
        for i in candidates:
            extra = min(limit - counts[i], max(1, left * loads[i] // whole), surplus)
            counts[i] = counts[i] + extra
            surplus = surplus - extra
    return np.array([limit] + counts)


def uneven(stream_key, number_of, total, most, lean):
    if number_of == 2:
        one = jax.random.randint(stream_key, (), max(1, total - most), min(most, total - 1) + 1)
        return jnp.stack([one, total - one])
    tallies = jnp.asarray(profile(number_of, total, most, lean), jnp.int32)
    pairs = (number_of - 1) // 2
    donor, taker = tallies[1:1 + 2 * pairs:2], tallies[2:2 + 2 * pairs:2]
    slack = jnp.minimum(donor - 1, most - taker)
    passed = jax.random.randint(jax.random.fold_in(stream_key, 1), (pairs,), 0, 1 << 20) % (slack + 1)
    tallies = tallies.at[1:1 + 2 * pairs:2].set(donor - passed).at[2:2 + 2 * pairs:2].set(taker + passed)
    return tallies[jax.random.permutation(jax.random.fold_in(stream_key, 2), number_of)]


def centred(stream_key, dims, scale, reach, cuts=(), kind=jnp.bfloat16):
    values = scale * jax.random.normal(stream_key, dims, jnp.float32)
    if cuts:
        values = values * steps_of(stream_key, dims, cuts, -0.22, 0.18)
    return jnp.clip(values, -reach, reach).astype(kind)


def setup_inputs(seed: int = 0) -> dict:
    arg_keys = jax.random.split(jax.random.key(seed), 14)
    image = draw_image(jax.random.fold_in(arg_keys[13], 71), 0)
    text = draw_text(jax.random.fold_in(arg_keys[13], 71), 0)
    pooled = centred(arg_keys[2], (REQS, D), 1.0, 6.0, ((0, 4),), jnp.float32)
    timesteps = place_ends(jax.random.randint(arg_keys[3], (REQS,), 0, 1000), jax.random.fold_in(arg_keys[3], 1), 0, 999).astype(jnp.int32)
    lengths = uneven(arg_keys[4], REQS, TOTAL, LMAX, 2).astype(jnp.int32)
    w_time = centred(arg_keys[5], (FREQ, D), FREQ ** -0.5, 0.375)
    w_mod = centred(arg_keys[6], (D, 4 * D), D ** -0.5, 0.125, ((1, 8),))
    w_img = centred(arg_keys[7], (D, 3 * HEADS * HD), D ** -0.5, 0.125, ((1, 32),))
    w_txt = centred(arg_keys[8], (D, 3 * HEADS * HD), D ** -0.5, 0.125, ((1, 8),))
    q_gain = jnp.clip(jnp.exp(jax.random.uniform(arg_keys[9], (HD,), jnp.float32, math.log(1.0), math.log(2.5))), 1.0, 2.5)
    k_gain = jnp.clip(jnp.exp(jax.random.uniform(arg_keys[10], (HD,), jnp.float32, math.log(1.0), math.log(2.5))), 1.0, 2.5)
    text_q_gain = jnp.clip(jnp.exp(jax.random.uniform(arg_keys[11], (HD,), jnp.float32, math.log(1.0), math.log(2.5))), 1.0, 2.5)
    text_k_gain = jnp.clip(jnp.exp(jax.random.uniform(arg_keys[12], (HD,), jnp.float32, math.log(1.0), math.log(2.5))), 1.0, 2.5)
    return {"image": image, "text": text, "pooled": pooled, "timesteps": timesteps, "lengths": lengths, "w_time": w_time, "w_mod": w_mod, "w_img": w_img, "w_txt": w_txt, "q_gain": q_gain, "k_gain": k_gain, "text_q_gain": text_q_gain, "text_k_gain": text_k_gain}


epsilon = 1e-06

def time_features(step_index, feature_count):
    half_count = feature_count // 2
    frequency = jnp.exp(-math.log(10000.0) * jnp.arange(half_count, dtype=jnp.float32) / half_count)
    angles = step_index.astype(jnp.float32)[:, None] * frequency[None, :]
    return jnp.concatenate([jnp.cos(angles), jnp.sin(angles)], axis=-1).astype(jnp.bfloat16)

def modulate(tokens, shift, scale):
    values = tokens.astype(jnp.float32)
    center = lax.optimization_barrier(jnp.mean(values, axis=-1, keepdims=True))
    spread = lax.optimization_barrier(jnp.mean(jnp.square(values - center), axis=-1, keepdims=True))
    normed = (values - center) * lax.rsqrt(spread + epsilon)
    return (normed * (1.0 + scale.astype(jnp.float32)) + shift.astype(jnp.float32)).astype(jnp.bfloat16)

def rms_gain(vectors, gain):
    factor = lax.rsqrt(lax.optimization_barrier(jnp.mean(jnp.square(vectors), axis=-1, keepdims=True)) + epsilon)
    return (vectors * factor * gain).astype(jnp.bfloat16)

def attend(queries, keys, values, key_mask):
    scores = jnp.einsum('qe,ke->qk', queries.astype(jnp.float32), keys.astype(jnp.float32)) * HD ** (-0.5)
    weights = jnp.exp(scores) * key_mask[None, :]
    total = lax.optimization_barrier(jnp.sum(weights, axis=-1))
    summed = jnp.dot(weights.astype(jnp.bfloat16), values, preferred_element_type=jnp.float32)
    return summed / total[:, None]

def reference(image, text, pooled, timesteps, lengths, w_time, w_mod, w_img, w_txt, q_gain, k_gain, text_q_gain, text_k_gain):
    features = time_features(timesteps, FREQ)
    cond_act = jax.nn.silu(pooled + jnp.dot(features, w_time, preferred_element_type=jnp.float32)).astype(jnp.bfloat16)
    modulation = jnp.dot(cond_act, w_mod, preferred_element_type=jnp.float32).astype(jnp.bfloat16)

    def one_request(operands):
        image_one, text_one, mod_one, length_one = operands
        slot_live = (jnp.arange(LMAX, dtype=jnp.int32) < length_one).astype(jnp.float32)
        key_mask = jnp.concatenate([jnp.ones((TXT,), jnp.float32), slot_live])
        h_img = modulate(image_one, mod_one[0:D], mod_one[D:2 * D])
        h_txt = modulate(text_one, mod_one[2 * D:3 * D], mod_one[3 * D:4 * D])
        qkv_img = jnp.dot(h_img, w_img, preferred_element_type=jnp.float32).reshape(LMAX, HEADS, 3, HD)
        qkv_txt = jnp.dot(h_txt, w_txt, preferred_element_type=jnp.float32).reshape(TXT, HEADS, 3, HD)
        queries = jnp.concatenate([rms_gain(qkv_txt[:, :, 0, :], text_q_gain), rms_gain(qkv_img[:, :, 0, :], q_gain)], axis=0)
        keys = jnp.concatenate([rms_gain(qkv_txt[:, :, 1, :], text_k_gain), rms_gain(qkv_img[:, :, 1, :], k_gain)], axis=0)
        values = jnp.concatenate([qkv_txt[:, :, 2, :].astype(jnp.bfloat16), qkv_img[:, :, 2, :].astype(jnp.bfloat16)], axis=0)

        def one_head(trio):
            return attend(trio[0], trio[1], trio[2], key_mask)
        outcome = lax.map(one_head, (jnp.moveaxis(queries, 1, 0), jnp.moveaxis(keys, 1, 0), jnp.moveaxis(values, 1, 0)))
        outcome = jnp.moveaxis(outcome, 0, 1).reshape(TXT + LMAX, HEADS * HD)
        text_result = outcome[:TXT].astype(jnp.bfloat16)
        image_result = (outcome[TXT:] * slot_live[:, None]).astype(jnp.bfloat16)
        return (image_result, text_result)
    image_attention, text_attention = lax.map(one_request, (image, text, modulation, lengths))
    return (image_attention, text_attention)
```

```python
import functools, math
import jax, jax.numpy as jnp
from jax import lax
from jax.experimental import pallas as pl
from jax.experimental.pallas import tpu as pltpu
from jax.sharding import PartitionSpec as P

def attend_kernel(block, tail, masked, len_ref, q_ref, k_ref, v_ref, tk_ref, tv_ref, *refs):
    rows = pl.program_id(1)
    length = len_ref[0]
    out_ref = refs[-1]
    many = out_ref.shape[0]
    chunks = length // block
    rest = (length - chunks * block + tail - 1) // tail
    half = q_ref.shape[1] // 2

    def weigh(queries, keys, values):
        scores = jnp.dot(keys, queries, preferred_element_type=jnp.float32)
        return jnp.dot(
            values, jnp.exp2(scores).astype(jnp.bfloat16), preferred_element_type=jnp.float32
        )

    def run(queries):
        def body(size, first, c, carry):
            here = pl.ds(pl.multiple_of(first + c * size, size), size)
            return tuple(
                carry[h] + weigh(queries, k_ref[h, here, :], v_ref[h, :, here]) for h in range(2)
            )

        carry = tuple(weigh(queries, tk_ref[h], tv_ref[h]) for h in range(2))
        carry = lax.fori_loop(0, chunks, functools.partial(body, block, 0), carry)
        carry = lax.fori_loop(0, rest, functools.partial(body, tail, chunks * block), carry)
        out = jnp.concatenate([sums[0:half] / sums[half : half + 1] for sums in carry], axis=0)
        return jnp.transpose(out)

    if not masked:
        out_ref[...] = run(q_ref[0]).astype(jnp.bfloat16)
        return

    @pl.when(rows * many < length)
    def _():
        result = run(q_ref[0])
        spot = rows * many + lax.broadcasted_iota(jnp.int32, result.shape, 0)
        out_ref[...] = jnp.where(spot < length, result, 0.0).astype(jnp.bfloat16)

    @pl.when(rows * many >= length)
    def _():
        out_ref[...] = jnp.zeros_like(out_ref)


def attend(length, q, k, v, tk, tv, first, last, seq, many, block, tail, masked, shared, earlier=None):
    pairs, width, rows = q.shape
    rows = min(rows, seq)
    text_keys = tk.shape[1]
    into = first if shared else 0
    operands = [length, q, k, v, tk, tv]
    aliases = {}
    if earlier is not None:
        aliases = {len(operands): 0}
        operands.append(earlier)
    columns = (pairs if shared else last - first) * width

    def live(r, s):
        return jnp.minimum(r, (s[0] + many - 1) // many - 1) if masked else r

    return pl.pallas_call(
        functools.partial(attend_kernel, block, tail, masked),
        grid_spec=pltpu.PrefetchScalarGridSpec(
            num_scalar_prefetch=1,
            grid=(last - first, rows // many),
            in_specs=[
                pl.BlockSpec((1, width, many), lambda p, r, s: (p + first, 0, live(r, s))),
                pl.BlockSpec((2, seq, width), lambda p, r, s: (p + first, 0, 0)),
                pl.BlockSpec((2, width, seq), lambda p, r, s: (p + first, 0, 0)),
                pl.BlockSpec((2, text_keys, width), lambda p, r, s: (p + first, 0, 0)),
                pl.BlockSpec((2, width, text_keys), lambda p, r, s: (p + first, 0, 0)),
            ]
            + [pl.BlockSpec(memory_space=pl.ANY) for _ in aliases],
            out_specs=pl.BlockSpec((many, width), lambda p, r, s: (r, p + into)),
        ),
        out_shape=jax.ShapeDtypeStruct((rows, columns), jnp.bfloat16),
        input_output_aliases=aliases,
        compiler_params=pltpu.CompilerParams(
            dimension_semantics=("arbitrary", "arbitrary"), vmem_limit_bytes=48 << 20
        ),
        cost_estimate=pl.CostEstimate(
            flops=(last - first) * 16 * rows * seq * width,
            bytes_accessed=(last - first) * 8 * seq * width,
            transcendentals=(last - first) * 2 * rows * seq,
        ),
        name="attend",
    )(*operands)


def arrange_kernel(head_dim, parts, order_ref, *refs):
    out_ref = refs[-1]
    width = 2 * head_dim
    tiles = refs[0].shape[0]
    start = 0
    for ref in refs[:parts]:
        for p in range(ref.shape[2] // width):
            for e in range(2):
                here = slice(p * width + e * head_dim, p * width + (e + 1) * head_dim)
                for a in range(tiles // 2):
                    both = [ref[2 * a, :, here], ref[2 * a + 1, :, here]]
                    out_ref[0, :, start : start + width] = jnp.concatenate(both, axis=1)
                    start += width


def arrange(place, parts, earlier, group_count, rows, head_dim):
    tiles, local_rows, _ = parts[0].shape
    operands = [place, *parts]
    aliases = {}
    if earlier is not None:
        aliases = {len(operands): 0}
        operands.append(earlier)
    total = sum(tiles * part.shape[2] for part in parts)
    return pl.pallas_call(
        functools.partial(arrange_kernel, head_dim, len(parts)),
        grid_spec=pltpu.PrefetchScalarGridSpec(
            num_scalar_prefetch=1,
            grid=(local_rows // rows,),
            in_specs=[
                pl.BlockSpec((tiles, rows, part.shape[2]), lambda r, s: (0, r, 0)) for part in parts
            ]
            + [pl.BlockSpec(memory_space=pl.ANY) for _ in aliases],
            out_specs=pl.BlockSpec((1, rows, total), lambda r, s: (s[0], r, 0)),
        ),
        out_shape=jax.ShapeDtypeStruct((group_count, local_rows, total), jnp.bfloat16),
        input_output_aliases=aliases,
        compiler_params=pltpu.CompilerParams(
            dimension_semantics=("arbitrary",), vmem_limit_bytes=48 << 20
        ),
        cost_estimate=pl.CostEstimate(
            flops=0, bytes_accessed=4 * local_rows * total, transcendentals=0
        ),
        name="arrange",
    )(*operands)


def project_kernel(head_dim, cover, arrays, chunks, spot_ref, *refs):
    x_refs = refs[:arrays]
    mod_ref, wq_ref, wk_ref, wv_ref, gain_ref, sum_ref = refs[arrays : arrays + 6]
    q_ref, k_ref, v_ref, held = refs[-4:]
    step = pl.program_id(0)
    rows = held.shape[0]
    length = spot_ref[chunks]
    spot = spot_ref[step]
    start = spot * rows

    @pl.when((spot >= 0) & (start < (length + cover - 1) // cover * cover))
    def _():
        if arrays == 1:
            x = x_refs[0][...].astype(jnp.float32)
        else:
            for i in range(arrays):

                @pl.when(step == i)
                def _():
                    held[...] = x_refs[i][...]

            x = held[...].astype(jnp.float32)
        depth = x.shape[1]
        center = jnp.sum(x, axis=1, keepdims=True) * (1.0 / depth)
        x = x - center
        spread = jnp.sum(x * x, axis=1, keepdims=True) * (1.0 / depth)
        h = x * lax.rsqrt(spread + epsilon)
        h = (h * (1.0 + mod_ref[1:2, :]) + mod_ref[0:1, :]).astype(jnp.bfloat16)

        def norm(values, gain):
            squares = values * values
            high = squares.astype(jnp.bfloat16)
            low = (squares - high.astype(jnp.float32)).astype(jnp.bfloat16)
            total = jnp.dot(high, sum_ref[...], preferred_element_type=jnp.float32)
            total = total + jnp.dot(low, sum_ref[...], preferred_element_type=jnp.float32)
            return (values * lax.rsqrt(total * (1.0 / head_dim) + epsilon) * gain).astype(
                jnp.bfloat16
            )

        width = 2 * head_dim
        q = norm(jnp.dot(h, wq_ref[...], preferred_element_type=jnp.float32), gain_ref[0:1, :])
        k = norm(jnp.dot(h, wk_ref[...], preferred_element_type=jnp.float32), gain_ref[1:2, :])
        v = jnp.dot(h, wv_ref[...], preferred_element_type=jnp.float32).astype(jnp.bfloat16)
        qt, vt = jnp.transpose(q), jnp.transpose(v)
        lane = lax.broadcasted_iota(jnp.int32, (rows, width), 1)
        live = start + lax.broadcasted_iota(jnp.int32, (head_dim, rows), 1) < length
        none = jnp.zeros((head_dim, rows), jnp.bfloat16)
        one = jnp.where(live, jnp.ones_like(none), none)
        gap = jnp.zeros((rows, width), jnp.bfloat16)
        for p in range(q.shape[1] // width):
            here = slice(p * width, (p + 1) * width)
            q_ref[p] = qt[here]
            k_ref[2 * p] = jnp.where(lane < head_dim, k[:, here], gap)
            k_ref[2 * p + 1] = jnp.where(lane < head_dim, gap, k[:, here])
            for h in (2 * p, 2 * p + 1):
                v_ref[h, 0:head_dim] = jnp.where(live, vt[h * head_dim : (h + 1) * head_dim], none)
                v_ref[h, head_dim:width] = one


def project(length, spots, tokens, mod, weights, gains, sums, seq, cover, head_dim, earlier):
    arrays, chunks = len(tokens), len(spots)
    depth = tokens[0].shape[1]
    rows = tokens[0].shape[0] * arrays // chunks
    cols = weights[0].shape[1]
    heads = cols // head_dim
    width = 2 * head_dim
    blocks = seq // rows
    scalars = jnp.concatenate([jnp.stack(spots).astype(jnp.int32), length])

    def place(i, s):
        spot = s[i]
        used = (spot >= 0) & (spot * rows < (s[chunks] + cover - 1) // cover * cover)
        return jnp.where(used, spot, blocks)

    def row(i, s):
        last = (s[chunks] + cover - 1) // cover * (cover // rows) - 1
        return (jnp.minimum(i, last) if arrays == 1 else 0, 0)

    def whole(a):
        return pl.BlockSpec(a.shape, lambda i, s: (0,) * a.ndim)

    constants = [mod, *weights, gains, sums]
    operands = [scalars, *tokens, *constants]
    aliases = {}
    if earlier is not None:
        aliases = {len(operands) + i: i for i in range(3)}
        operands += list(earlier)
    padded = seq + max(rows, 128)
    return pl.pallas_call(
        functools.partial(project_kernel, head_dim, cover, arrays, chunks),
        grid_spec=pltpu.PrefetchScalarGridSpec(
            num_scalar_prefetch=1,
            grid=(chunks,),
            in_specs=[pl.BlockSpec((rows, depth), row) for _ in tokens]
            + [whole(a) for a in constants]
            + [pl.BlockSpec(memory_space=pl.ANY) for _ in aliases],
            out_specs=[
                pl.BlockSpec((heads // 2, width, rows), lambda i, s: (0, 0, place(i, s))),
                pl.BlockSpec((heads, rows, width), lambda i, s: (0, place(i, s), 0)),
                pl.BlockSpec((heads, width, rows), lambda i, s: (0, 0, place(i, s))),
            ],
            scratch_shapes=[pltpu.VMEM((rows, depth), jnp.bfloat16)],
        ),
        out_shape=[
            jax.ShapeDtypeStruct((heads // 2, width, padded), jnp.bfloat16),
            jax.ShapeDtypeStruct((heads, padded, width), jnp.bfloat16),
            jax.ShapeDtypeStruct((heads, width, padded), jnp.bfloat16),
        ],
        input_output_aliases=aliases,
        compiler_params=pltpu.CompilerParams(
            dimension_semantics=("arbitrary",), vmem_limit_bytes=48 << 20
        ),
        cost_estimate=pl.CostEstimate(
            flops=6 * chunks * rows * depth * cols,
            bytes_accessed=2 * (chunks * rows * depth + 3 * depth * cols),
            transcendentals=chunks * rows,
        ),
        name="project",
    )(*operands)


epsilon = 1e-06


def time_features(step_index, feature_count):
    half_count = feature_count // 2
    frequency = jnp.exp(-math.log(10000.0) * jnp.arange(half_count, dtype=jnp.float32) / half_count)
    angles = step_index.astype(jnp.float32)[:, None] * frequency[None, :]
    return jnp.concatenate([jnp.cos(angles), jnp.sin(angles)], axis=-1).astype(jnp.bfloat16)


def modulate(tokens, shift, scale):
    values = tokens.astype(jnp.float32)
    center = jnp.mean(values, axis=-1, keepdims=True)
    spread = jnp.mean(jnp.square(values - center), axis=-1, keepdims=True)
    normed = (values - center) * lax.rsqrt(spread + epsilon)
    return (normed * (1.0 + scale.astype(jnp.float32)) + shift.astype(jnp.float32)).astype(
        jnp.bfloat16
    )


def rms_gain(vectors, gain):
    factor = lax.rsqrt(jnp.mean(jnp.square(vectors), axis=-1, keepdims=True) + epsilon)
    return (vectors * factor * gain).astype(jnp.bfloat16)


def gather_req(shard):
    count = lax.axis_size("req")
    if count & (count - 1):
        return lax.all_gather(shard, "req", axis=0)
    mine = lax.axis_index("req")
    shards = [shard]
    for step in range(1, count):
        shards.append(lax.ppermute(shard, "req", [(i, i ^ step) for i in range(count)]))
    stacked = jnp.stack(shards)
    return jnp.stack(
        [lax.dynamic_index_in_dim(stacked, mine ^ i, 0, keepdims=False) for i in range(count)]
    )


def head_weights(w_img, head_dim, heads_here):
    width = 3 * head_dim
    if strided(w_img, head_dim, heads_here):
        shards = gather_req(w_img)
        depth = shards.shape[1]
        shards = shards.reshape(heads_here, depth, 3, head_dim)
    else:
        whole = lax.all_gather(w_img, ("req", "tile"), axis=1, tiled=True)
        depth = whole.shape[0]
        start = lax.axis_index("tile") * heads_here * width
        part = lax.dynamic_slice_in_dim(whole, start, heads_here * width, axis=1)
        shards = jnp.moveaxis(part.reshape(depth, heads_here, 3, head_dim), 1, 0)
    shards = jnp.pad(shards, ((0, heads_here % 2), (0, 0), (0, 0), (0, 0)))
    return jnp.transpose(shards, (2, 1, 0, 3)).reshape(3, depth, -1)


def strided(w_img, head_dim, heads_here):
    return (
        w_img.shape[1] == 3 * head_dim
        and heads_here == lax.axis_size("req")
        and lax.axis_size("tile") % heads_here == 0
    )


def text_to_strided(qkv):
    tiles, mine, heads = lax.axis_size("tile"), lax.axis_index("tile"), qkv.shape[2]
    folds = tiles // heads
    parts = jnp.moveaxis(qkv, 2, 0)
    pick = (jnp.arange(folds) == mine % folds)[:, None, None, None, None]
    send = jnp.where(pick, parts[None], jnp.zeros_like(parts[None]))
    send = send.reshape((tiles,) + parts.shape[1:])
    got = lax.all_to_all(send, "tile", split_axis=0, concat_axis=0, tiled=True)
    got = got.reshape((heads, folds) + parts.shape[1:])
    return jnp.moveaxis(
        lax.dynamic_index_in_dim(got, mine // heads, 1, keepdims=False), 0, 2
    )


def text_from_strided(out, head_dim):
    tiles, mine = lax.axis_size("tile"), lax.axis_index("tile")
    groups, text_len, width = out.shape
    heads = width // head_dim
    folds = tiles // heads
    parts = jnp.moveaxis(out.reshape(groups, text_len, heads, head_dim), 2, 0)
    pick = (jnp.arange(folds) == mine // heads)[None, :, None, None, None]
    send = jnp.where(pick, parts[:, None], jnp.zeros_like(parts[:, None]))
    send = send.reshape((tiles,) + parts.shape[1:])
    got = lax.all_to_all(send, "tile", split_axis=0, concat_axis=0, tiled=True)
    got = got.reshape((folds, heads) + parts.shape[1:])
    got = lax.dynamic_index_in_dim(got, mine % folds, 0, keepdims=False)
    return jnp.moveaxis(got, 0, 2).reshape(groups, text_len, width)


def after(values, *others):
    return lax.optimization_barrier((values, others))[0]


class Spread:
    def __init__(self, tokens):
        self.tiles, self.mine = lax.axis_size("tile"), lax.axis_index("tile")
        self.pair = 2 if self.tiles % 2 == 0 else 1
        self.steps = self.tiles // self.pair
        self.right = self.left = tokens
        self.done = 0
        self.found = [self.both(tokens, self.mine)]

    def both(self, chunk, source):
        valid = (source >= 0) & (source < self.tiles)
        found = [(chunk, jnp.where(valid, source, -1))]
        if self.pair == 2:
            source = source + 1 - 2 * (self.mine % 2)
            swap = [(i, i ^ 1) for i in range(self.tiles)]
            found.append((lax.ppermute(chunk, "tile", swap), jnp.where(valid, source, -1)))
        return found

    def step(self, *others):
        if others:
            self.right, self.left = after((self.right, self.left), *others)
        pairs = [(i, i + self.pair) for i in range(self.tiles - self.pair)]
        self.right = lax.ppermute(self.right, "tile", pairs)
        self.left = lax.ppermute(self.left, "tile", [(j, i) for i, j in pairs])
        self.done += 1
        offset = self.pair * self.done
        self.found.append(
            self.both(self.right, self.mine - offset) + self.both(self.left, self.mine + offset)
        )


def text_operands(qkv, head_dim, rows, keys):
    text_len, heads = qkv.shape[0], qkv.shape[1]
    turned = jnp.transpose(qkv, (1, 2, 0))
    queries = turned[:, 0:head_dim].reshape(heads // 2, 2 * head_dim, text_len)
    queries = jnp.pad(queries, ((0, 0), (0, 0), (0, rows - text_len)))
    even = (jnp.arange(heads) % 2 == 0)[:, None, None]
    key = jnp.moveaxis(qkv[:, :, head_dim : 2 * head_dim], 1, 0)
    none = jnp.zeros_like(key)
    key = jnp.concatenate([jnp.where(even, key, none), jnp.where(even, none, key)], axis=2)
    key = jnp.pad(key, ((0, 0), (0, keys - text_len), (0, 0)))
    value = turned[:, 2 * head_dim : 3 * head_dim]
    value = jnp.concatenate([value, jnp.ones_like(value)], axis=1)
    value = jnp.pad(value, ((0, 0), (0, 0), (0, keys - text_len)))
    return queries, key, value


def local(
    image,
    text,
    pooled,
    timesteps,
    lengths,
    w_time,
    w_mod,
    w_img,
    w_txt,
    q_gain,
    k_gain,
    text_q_gain,
    text_k_gain,
):
    tiles = lax.axis_size("tile")
    group_count, local_rows, model_width = image.shape
    seq_len = local_rows * tiles
    text_len = text.shape[1]
    head_dim = q_gain.shape[0]
    heads_here = w_txt.shape[1] // (3 * head_dim)
    spare = heads_here % 2
    width = (heads_here + spare) * head_dim
    query_factor = head_dim ** (-0.5) * math.log2(math.e)
    text_rows = -(-text_len // 128) * 128
    text_keys = -(-text_len // 128) * 128
    by_stride = strided(w_img, head_dim, heads_here)

    if group_count == 2:
        longer = (lengths[1] > lengths[0]).astype(jnp.int32)
        order = undo = jnp.stack([longer, 1 - longer])
    else:
        order = jnp.argsort(-lengths)
        undo = jnp.argsort(order)
    sorted_lengths = lengths[order]
    tokens = [
        lax.dynamic_index_in_dim(image, order[slot], 0, keepdims=False)
        for slot in range(group_count)
    ]
    first = Spread(tokens[0])
    first.step()

    features = time_features(timesteps, w_time.shape[0])
    cond_act = jax.nn.silu(
        pooled + jnp.dot(features, w_time, preferred_element_type=jnp.float32)
    ).astype(jnp.bfloat16)
    mod_part = jnp.dot(cond_act, w_mod, preferred_element_type=jnp.float32).astype(jnp.bfloat16)
    modulation = lax.all_to_all(
        jnp.broadcast_to(mod_part[None], (tiles,) + mod_part.shape),
        "tile",
        split_axis=0,
        concat_axis=0,
        tiled=True,
    )
    modulation = jnp.moveaxis(modulation, 0, 1)
    modulation = modulation.reshape(group_count, 4, model_width)

    weights = head_weights(w_img, head_dim, heads_here)
    gains = jnp.stack(
        [
            jnp.tile(q_gain * query_factor, heads_here + spare),
            jnp.tile(k_gain, heads_here + spare),
        ]
    )
    group_of = jnp.arange(width) // head_dim
    sums = (group_of[:, None] == group_of[None, :]).astype(jnp.bfloat16)

    h_txt = modulate(text, modulation[:, None, 2], modulation[:, None, 3])
    qkv_txt = jnp.einsum("gtd,dc->gtc", h_txt, w_txt, preferred_element_type=jnp.float32).reshape(
        group_count, text_len, heads_here, 3, head_dim
    )
    text_qkv = jnp.concatenate(
        [
            rms_gain(qkv_txt[:, :, :, 0, :], text_q_gain * query_factor),
            rms_gain(qkv_txt[:, :, :, 1, :], text_k_gain),
            qkv_txt[:, :, :, 2, :].astype(jnp.bfloat16),
        ],
        axis=-1,
    )
    local_text = text_qkv
    if by_stride:
        text_qkv = text_to_strided(text_qkv)
    text_qkv = jnp.pad(text_qkv, ((0, 0), (0, 0), (0, spare), (0, 0)))

    cover = min(512, seq_len)
    block = min(1024, seq_len)
    pairs = width // (2 * head_dim)
    lengths_of, mods, text_parts = [], [], []
    for slot in range(group_count):
        lengths_of.append(lax.dynamic_slice_in_dim(sorted_lengths, slot, 1))
        mod = lax.dynamic_index_in_dim(modulation, order[slot], 0, keepdims=False)
        mods.append(mod[0:2].astype(jnp.float32))
        one = lax.dynamic_index_in_dim(text_qkv, order[slot], 0, keepdims=False)
        text_parts.append(text_operands(one, head_dim, text_rows, text_keys))

    def project_step(slot, found, earlier):
        return project(
            lengths_of[slot],
            [source for _, source in found],
            [chunk for chunk, _ in found],
            mods[slot],
            [weights[i] for i in range(3)],
            gains,
            sums,
            seq_len,
            cover,
            head_dim,
            earlier,
        )

    def attend_text(slot, packed):
        query, key, value = text_parts[slot]
        operands = (lengths_of[slot], query, packed[1], packed[2], key, value)
        out = attend(*operands, 0, pairs, seq_len, text_rows, block, cover, False, True)
        return out[0:text_len, 0 : heads_here * head_dim]

    def attend_image(slot, packed, start, stop, many, shared, earlier=None):
        _, key, value = text_parts[slot]
        operands = (lengths_of[slot], *packed, key, value)
        return attend(
            *operands, start, stop, seq_len, many, block, cover, True, shared, earlier
        )

    def send_back(out):
        out = out[:, 0 : heads_here * head_dim].reshape(tiles, local_rows, -1)
        return lax.all_to_all(out, "tile", split_axis=0, concat_axis=0, tiled=True)

    image_attention = None
    image_back, text_outs = [], []
    spreading = first
    waiting = [mod_part]
    packed = None
    for slot in range(group_count):
        latest = slot == group_count - 1
        if slot > 0:
            following = Spread(after(tokens[slot], spreading.right, spreading.left))
            following.step(packed)
            waiting = []
            previous, before = packed, spreading
            for found in before.found[consumed:]:
                previous = project_step(slot - 1, found, previous)
            waiting.append([previous])
            out = None
            for pair in range(pairs):
                out = attend_image(slot - 1, previous, pair, pair + 1, block, True, out)
                waiting.append([out])
            text_outs.append(attend_text(slot - 1, previous))
            image_back.append([send_back(out)])
            spreading = following
            packed = None
            consumed = 0
            for step in range(2, spreading.steps):
                spreading.step(*(waiting[step - 2] if step - 2 < len(waiting) else []))
            packed = project_step(slot, after(spreading.found[0], *waiting[-1]), None)
            consumed = 1
        else:
            spreading.step(mod_part)
            for step in range(3, spreading.steps):
                spreading.step(*([weights, local_text] if step == 3 else []))
            packed = project_step(slot, spreading.found[0], None)
            packed = project_step(slot, spreading.found[1], packed)
            consumed = 2
        if latest:
            for found in spreading.found[consumed:]:
                packed = project_step(slot, found, packed)
            text_outs.append(attend_text(slot, packed))
            text_attention = jnp.stack(text_outs)[undo]
            if by_stride:
                text_attention = text_from_strided(text_attention, head_dim)
            parts = []
            for pair in range(pairs):
                out = attend_image(slot, packed, pair, pair + 1, cover, False)
                parts.append(send_back(out))
            image_back.append(parts)

    if by_stride:
        for slot, parts in enumerate(image_back):
            place = lax.dynamic_slice_in_dim(order, slot, 1)
            image_attention = arrange(
                place, parts, image_attention, group_count, min(128, local_rows), head_dim
            )
    else:
        image_attention = jnp.stack(
            [
                jnp.concatenate(
                    [part.reshape(tiles, local_rows, -1, head_dim) for part in parts], axis=2
                )
                for parts in image_back
            ]
        )[undo]
        image_attention = jnp.transpose(image_attention, (0, 2, 1, 3, 4)).reshape(
            group_count, local_rows, tiles * heads_here * head_dim
        )
    return (image_attention, text_attention)


def solution(mesh):
    in_specs = (
        P("req", "tile", None),
        P("req", None, None),
        P("req", None),
        P("req"),
        P("req"),
        P(),
        P(None, "tile"),
        P(None, ("req", "tile")),
        P(None, "tile"),
        P(),
        P(),
        P(),
        P(),
    )
    out_specs = (P("req", "tile", None), P("req", None, "tile"))
    return jax.shard_map(local, mesh=mesh, in_specs=in_specs, out_specs=out_specs, check_vma=False)
```

```python
import functools, math
import jax, jax.numpy as jnp
from jax import lax
from jax.experimental import pallas as pl
from jax.experimental.pallas import tpu as pltpu
from jax.sharding import PartitionSpec as P

def attend_kernel(block, tail, masked, len_ref, q_ref, k_ref, v_ref, tk_ref, tv_ref, *refs):
    rows = pl.program_id(1)
    length = len_ref[0]
    out_ref = refs[-1]
    many = out_ref.shape[0]
    chunks = length // block
    rest = (length - chunks * block + tail - 1) // tail
    half = q_ref.shape[1] // 2

    def weigh(queries, keys, values):
        scores = jnp.dot(keys, queries, preferred_element_type=jnp.float32)
        return jnp.dot(
            values, jnp.exp2(scores).astype(jnp.bfloat16), preferred_element_type=jnp.float32
        )

    def run(queries):
        def body(size, first, c, carry):
            here = pl.ds(pl.multiple_of(first + c * size, size), size)
            return tuple(
                carry[h] + weigh(queries, k_ref[h, here, :], v_ref[h, :, here]) for h in range(2)
            )

        carry = tuple(weigh(queries, tk_ref[h], tv_ref[h]) for h in range(2))
        carry = lax.fori_loop(0, chunks, functools.partial(body, block, 0), carry)
        carry = lax.fori_loop(0, rest, functools.partial(body, tail, chunks * block), carry)
        out = jnp.concatenate([sums[0:half] / sums[half : half + 1] for sums in carry], axis=0)
        return jnp.transpose(out)

    if not masked:
        out_ref[...] = run(q_ref[0]).astype(jnp.bfloat16)
        return

    @pl.when(rows * many < length)
    def _():
        result = run(q_ref[0])
        spot = rows * many + lax.broadcasted_iota(jnp.int32, result.shape, 0)
        out_ref[...] = jnp.where(spot < length, result, 0.0).astype(jnp.bfloat16)

    @pl.when(rows * many >= length)
    def _():
        out_ref[...] = jnp.zeros_like(out_ref)


def attend(length, q, k, v, tk, tv, first, last, seq, many, block, tail, masked, shared, earlier=None):
    pairs, width, rows = q.shape
    rows = min(rows, seq)
    text_keys = tk.shape[1]
    into = first if shared else 0
    operands = [length, q, k, v, tk, tv]
    aliases = {}
    if earlier is not None:
        aliases = {len(operands): 0}
        operands.append(earlier)
    columns = (pairs if shared else last - first) * width

    def live(r, s):
        return jnp.minimum(r, (s[0] + many - 1) // many - 1) if masked else r

    return pl.pallas_call(
        functools.partial(attend_kernel, block, tail, masked),
        grid_spec=pltpu.PrefetchScalarGridSpec(
            num_scalar_prefetch=1,
            grid=(last - first, rows // many),
            in_specs=[
                pl.BlockSpec((1, width, many), lambda p, r, s: (p + first, 0, live(r, s))),
                pl.BlockSpec((2, seq, width), lambda p, r, s: (p + first, 0, 0)),
                pl.BlockSpec((2, width, seq), lambda p, r, s: (p + first, 0, 0)),
                pl.BlockSpec((2, text_keys, width), lambda p, r, s: (p + first, 0, 0)),
                pl.BlockSpec((2, width, text_keys), lambda p, r, s: (p + first, 0, 0)),
            ]
            + [pl.BlockSpec(memory_space=pl.ANY) for _ in aliases],
            out_specs=pl.BlockSpec((many, width), lambda p, r, s: (r, p + into)),
        ),
        out_shape=jax.ShapeDtypeStruct((rows, columns), jnp.bfloat16),
        input_output_aliases=aliases,
        compiler_params=pltpu.CompilerParams(
            dimension_semantics=("arbitrary", "arbitrary"), vmem_limit_bytes=48 << 20
        ),
        cost_estimate=pl.CostEstimate(flops=0, bytes_accessed=8 << 20, transcendentals=0),
        name="attend",
    )(*operands)


def arrange_kernel(head_dim, parts, order_ref, *refs):
    out_ref = refs[-1]
    width = 2 * head_dim
    tiles = refs[0].shape[0]
    start = 0
    for ref in refs[:parts]:
        for p in range(ref.shape[2] // width):
            for e in range(2):
                here = slice(p * width + e * head_dim, p * width + (e + 1) * head_dim)
                for a in range(tiles // 2):
                    both = [ref[2 * a, :, here], ref[2 * a + 1, :, here]]
                    out_ref[0, :, start : start + width] = jnp.concatenate(both, axis=1)
                    start += width


def arrange(place, parts, earlier, group_count, rows, head_dim):
    tiles, local_rows, _ = parts[0].shape
    operands = [place, *parts]
    aliases = {}
    if earlier is not None:
        aliases = {len(operands): 0}
        operands.append(earlier)
    total = sum(tiles * part.shape[2] for part in parts)
    return pl.pallas_call(
        functools.partial(arrange_kernel, head_dim, len(parts)),
        grid_spec=pltpu.PrefetchScalarGridSpec(
            num_scalar_prefetch=1,
            grid=(local_rows // rows,),
            in_specs=[
                pl.BlockSpec((tiles, rows, part.shape[2]), lambda r, s: (0, r, 0)) for part in parts
            ]
            + [pl.BlockSpec(memory_space=pl.ANY) for _ in aliases],
            out_specs=pl.BlockSpec((1, rows, total), lambda r, s: (s[0], r, 0)),
        ),
        out_shape=jax.ShapeDtypeStruct((group_count, local_rows, total), jnp.bfloat16),
        input_output_aliases=aliases,
        compiler_params=pltpu.CompilerParams(
            dimension_semantics=("arbitrary",), vmem_limit_bytes=48 << 20
        ),
        cost_estimate=pl.CostEstimate(
            flops=0, bytes_accessed=4 * local_rows * total, transcendentals=0
        ),
        name="arrange",
    )(*operands)


def project_kernel(head_dim, cover, chunks, spot_ref, *refs):
    x_refs = refs[:chunks]
    mod_ref, wq_ref, wk_ref, wv_ref, gain_ref, sum_ref = refs[chunks : chunks + 6]
    q_ref, k_ref, v_ref, x_buf, held, sems = refs[-6:]
    step = pl.program_id(0)
    rows, depth = held.shape
    length = spot_ref[chunks]
    start = spot_ref[step] * rows
    part = min(256, rows)
    group = 16

    def used(i):
        spot = spot_ref[i]
        return (spot >= 0) & (spot * rows < (length + cover - 1) // cover * cover)

    @pl.when(step == 0)
    def _():
        for i in range(chunks):

            @pl.when(used(i))
            def _():
                pltpu.make_async_copy(x_refs[i], x_buf.at[i], sems.at[i]).start()

    @pl.when(used(step))
    def _():
        pltpu.make_async_copy(x_refs[0], x_buf.at[step], sems.at[step]).wait()

        def normalize(base):
            for first in range(base, base + part, group):
                here = slice(first, first + group)
                x = x_buf[step, here, :].astype(jnp.float32)
                x = x - jnp.sum(x, axis=1, keepdims=True) * (1.0 / depth)
                spread = jnp.sum(x * x, axis=1, keepdims=True) * (1.0 / depth)
                h = x * lax.rsqrt(spread + epsilon)
                h = h * (1.0 + mod_ref[1:2, :]) + mod_ref[0:1, :]
                held[here, :] = h.astype(jnp.bfloat16)

        def norm(values, gain):
            squares = values * values
            high = squares.astype(jnp.bfloat16)
            low = (squares - high.astype(jnp.float32)).astype(jnp.bfloat16)
            total = jnp.dot(high, sum_ref[...], preferred_element_type=jnp.float32)
            total = total + jnp.dot(low, sum_ref[...], preferred_element_type=jnp.float32)
            return (values * lax.rsqrt(total * (1.0 / head_dim) + epsilon) * gain).astype(
                jnp.bfloat16
            )

        def product(base, w_ref):
            return jnp.dot(
                held[base : base + part, :], w_ref[...], preferred_element_type=jnp.float32
            )

        width = 2 * head_dim
        queries, keys, values = [], [], []
        normalize(0)
        for base in range(0, rows, part):
            if base + part < rows:
                normalize(base + part)
            query, key, value = [product(base, w) for w in (wq_ref, wk_ref, wv_ref)]
            queries.append(norm(query, gain_ref[0:1, :]))
            keys.append(norm(key, gain_ref[1:2, :]))
            values.append(value.astype(jnp.bfloat16))
        q, k, v = [jnp.concatenate(a, axis=0) for a in (queries, keys, values)]
        qt, vt = jnp.transpose(q), jnp.transpose(v)
        lane = lax.broadcasted_iota(jnp.int32, (rows, width), 1)
        live = start + lax.broadcasted_iota(jnp.int32, (head_dim, rows), 1) < length
        none = jnp.zeros((head_dim, rows), jnp.bfloat16)
        one = jnp.where(live, jnp.ones_like(none), none)
        gap = jnp.zeros((rows, width), jnp.bfloat16)
        for p in range(q.shape[1] // width):
            here = slice(p * width, (p + 1) * width)
            q_ref[p] = qt[here]
            k_ref[2 * p] = jnp.where(lane < head_dim, k[:, here], gap)
            k_ref[2 * p + 1] = jnp.where(lane < head_dim, gap, k[:, here])
            for h in (2 * p, 2 * p + 1):
                v_ref[h, 0:head_dim] = jnp.where(live, vt[h * head_dim : (h + 1) * head_dim], none)
                v_ref[h, head_dim:width] = one


def project(length, spots, tokens, mod, weights, gains, sums, seq, cover, head_dim, earlier):
    chunks = len(tokens)
    rows, depth = tokens[0].shape
    cols = weights[0].shape[1]
    heads = cols // head_dim
    width = 2 * head_dim
    blocks = seq // rows
    scalars = jnp.concatenate([jnp.stack(spots).astype(jnp.int32), length])

    def place(i, s):
        spot = s[i]
        used = (spot >= 0) & (spot * rows < (s[chunks] + cover - 1) // cover * cover)
        return jnp.where(used, spot, blocks)

    def whole(a):
        return pl.BlockSpec(a.shape, lambda i, s: (0,) * a.ndim)

    constants = [mod, *weights, gains, sums]
    operands = [scalars, *tokens, *constants]
    aliases = {}
    if earlier is not None:
        aliases = {len(operands) + i: i for i in range(3)}
        operands += list(earlier)
    padded = seq + max(rows, 128)
    return pl.pallas_call(
        functools.partial(project_kernel, head_dim, cover, chunks),
        grid_spec=pltpu.PrefetchScalarGridSpec(
            num_scalar_prefetch=1,
            grid=(chunks,),
            in_specs=[pl.BlockSpec(memory_space=pl.ANY) for _ in tokens]
            + [whole(a) for a in constants]
            + [pl.BlockSpec(memory_space=pl.ANY) for _ in aliases],
            out_specs=[
                pl.BlockSpec((heads // 2, width, rows), lambda i, s: (0, 0, place(i, s))),
                pl.BlockSpec((heads, rows, width), lambda i, s: (0, place(i, s), 0)),
                pl.BlockSpec((heads, width, rows), lambda i, s: (0, 0, place(i, s))),
            ],
            scratch_shapes=[
                pltpu.VMEM((chunks, rows, depth), jnp.bfloat16),
                pltpu.VMEM((rows, depth), jnp.bfloat16),
                pltpu.SemaphoreType.DMA((chunks,)),
            ],
        ),
        out_shape=[
            jax.ShapeDtypeStruct((heads // 2, width, padded), jnp.bfloat16),
            jax.ShapeDtypeStruct((heads, padded, width), jnp.bfloat16),
            jax.ShapeDtypeStruct((heads, width, padded), jnp.bfloat16),
        ],
        input_output_aliases=aliases,
        compiler_params=pltpu.CompilerParams(
            dimension_semantics=("arbitrary",), vmem_limit_bytes=48 << 20
        ),
        cost_estimate=pl.CostEstimate(flops=0, bytes_accessed=1 << 20, transcendentals=0),
        name="project",
    )(*operands)


epsilon = 1e-06


def time_features(step_index, feature_count):
    half_count = feature_count // 2
    frequency = jnp.exp(-math.log(10000.0) * jnp.arange(half_count, dtype=jnp.float32) / half_count)
    angles = step_index.astype(jnp.float32)[:, None] * frequency[None, :]
    return jnp.concatenate([jnp.cos(angles), jnp.sin(angles)], axis=-1).astype(jnp.bfloat16)


def modulate(tokens, shift, scale):
    values = tokens.astype(jnp.float32)
    center = jnp.mean(values, axis=-1, keepdims=True)
    spread = jnp.mean(jnp.square(values - center), axis=-1, keepdims=True)
    normed = (values - center) * lax.rsqrt(spread + epsilon)
    return (normed * (1.0 + scale.astype(jnp.float32)) + shift.astype(jnp.float32)).astype(
        jnp.bfloat16
    )


def rms_gain(vectors, gain):
    factor = lax.rsqrt(jnp.mean(jnp.square(vectors), axis=-1, keepdims=True) + epsilon)
    return (vectors * factor * gain).astype(jnp.bfloat16)


def head_weights(w_img, head_dim, heads_here):
    width = 3 * head_dim
    if strided(w_img, head_dim, heads_here):
        shards = lax.all_gather(w_img, "req", axis=0)
        depth = shards.shape[1]
        shards = shards.reshape(heads_here, depth, 3, head_dim)
    else:
        whole = lax.all_gather(w_img, ("req", "tile"), axis=1, tiled=True)
        depth = whole.shape[0]
        start = lax.axis_index("tile") * heads_here * width
        part = lax.dynamic_slice_in_dim(whole, start, heads_here * width, axis=1)
        shards = jnp.moveaxis(part.reshape(depth, heads_here, 3, head_dim), 1, 0)
    shards = jnp.pad(shards, ((0, heads_here % 2), (0, 0), (0, 0), (0, 0)))
    return jnp.transpose(shards, (2, 1, 0, 3)).reshape(3, depth, -1)


def strided(w_img, head_dim, heads_here):
    return (
        w_img.shape[1] == 3 * head_dim
        and heads_here == lax.axis_size("req")
        and lax.axis_size("tile") % heads_here == 0
    )


def text_to_send(qkv):
    tiles, mine, heads = lax.axis_size("tile"), lax.axis_index("tile"), qkv.shape[2]
    folds = tiles // heads
    parts = jnp.moveaxis(qkv, 2, 0)
    pick = (jnp.arange(folds) == mine % folds)[:, None, None, None, None]
    send = jnp.where(pick, parts[None], jnp.zeros_like(parts[None]))
    return lax.optimization_barrier(send.reshape((tiles,) + parts.shape[1:]))


def text_to_strided(send, heads):
    tiles, mine = lax.axis_size("tile"), lax.axis_index("tile")
    folds = tiles // heads
    got = lax.all_to_all(send, "tile", split_axis=0, concat_axis=0, tiled=True)
    got = got.reshape((heads, folds) + send.shape[1:])
    return jnp.moveaxis(
        lax.dynamic_index_in_dim(got, mine // heads, 1, keepdims=False), 0, 2
    )


def text_from_strided(out, head_dim):
    tiles, mine = lax.axis_size("tile"), lax.axis_index("tile")
    groups, text_len, width = out.shape
    heads = width // head_dim
    folds = tiles // heads
    parts = jnp.moveaxis(out.reshape(groups, text_len, heads, head_dim), 2, 0)
    got = lax.all_gather(parts, "tile", axis=0)
    got = got.reshape((folds, heads, heads) + parts.shape[1:])
    got = lax.dynamic_index_in_dim(got, mine % folds, 0, keepdims=False)
    got = lax.dynamic_index_in_dim(got, mine // folds, 1, keepdims=False)
    return jnp.moveaxis(got, 0, 2).reshape(groups, text_len, width)


def after(values, *others):
    return lax.optimization_barrier((values, others))[0]


class Spread:
    def __init__(self, tokens):
        self.tiles, self.mine = lax.axis_size("tile"), lax.axis_index("tile")
        self.pair = 2 if self.tiles % 2 == 0 else 1
        self.steps = self.tiles // self.pair
        self.right = self.left = tokens
        self.done = 0
        self.found = [self.both(tokens, self.mine)]

    def both(self, chunk, source):
        valid = (source >= 0) & (source < self.tiles)
        found = [(chunk, jnp.where(valid, source, -1))]
        if self.pair == 2:
            source = source + 1 - 2 * (self.mine % 2)
            swap = [(i, i ^ 1) for i in range(self.tiles)]
            found.append((lax.ppermute(chunk, "tile", swap), jnp.where(valid, source, -1)))
        return found

    def step(self):
        pairs = [(i, i + self.pair) for i in range(self.tiles - self.pair)]
        self.right = lax.ppermute(self.right, "tile", pairs)
        self.left = lax.ppermute(self.left, "tile", [(j, i) for i, j in pairs])
        self.done += 1

    def join(self, *others):
        self.right, self.left = after((self.right, self.left), *others)
        offset = self.pair * self.done
        self.found.append(
            self.both(self.right, self.mine - offset) + self.both(self.left, self.mine + offset)
        )


def text_operands(qkv, head_dim, rows, keys):
    text_len, heads = qkv.shape[0], qkv.shape[1]
    turned = jnp.transpose(qkv, (1, 2, 0))
    queries = turned[:, 0:head_dim].reshape(heads // 2, 2 * head_dim, text_len)
    queries = jnp.pad(queries, ((0, 0), (0, 0), (0, rows - text_len)))
    even = (jnp.arange(heads) % 2 == 0)[:, None, None]
    key = jnp.moveaxis(qkv[:, :, head_dim : 2 * head_dim], 1, 0)
    none = jnp.zeros_like(key)
    key = jnp.concatenate([jnp.where(even, key, none), jnp.where(even, none, key)], axis=2)
    key = jnp.pad(key, ((0, 0), (0, keys - text_len), (0, 0)))
    value = turned[:, 2 * head_dim : 3 * head_dim]
    value = jnp.concatenate([value, jnp.ones_like(value)], axis=1)
    value = jnp.pad(value, ((0, 0), (0, 0), (0, keys - text_len)))
    return queries, key, value


def local(
    image,
    text,
    pooled,
    timesteps,
    lengths,
    w_time,
    w_mod,
    w_img,
    w_txt,
    q_gain,
    k_gain,
    text_q_gain,
    text_k_gain,
):
    tiles = lax.axis_size("tile")
    group_count, local_rows, model_width = image.shape
    seq_len = local_rows * tiles
    text_len = text.shape[1]
    head_dim = q_gain.shape[0]
    heads_here = w_txt.shape[1] // (3 * head_dim)
    spare = heads_here % 2
    width = (heads_here + spare) * head_dim
    query_factor = head_dim ** (-0.5) * math.log2(math.e)
    text_rows = -(-text_len // 128) * 128
    text_keys = -(-text_len // 128) * 128
    by_stride = strided(w_img, head_dim, heads_here)

    if group_count == 2:
        longer = (lengths[1] > lengths[0]).astype(jnp.int32)
        order = undo = jnp.stack([longer, 1 - longer])
    else:
        order = jnp.argsort(-lengths)
        undo = jnp.argsort(order)
    sorted_lengths = lengths[order]
    tokens = [
        lax.dynamic_index_in_dim(image, order[slot], 0, keepdims=False)
        for slot in range(group_count)
    ]
    first = Spread(tokens[0])
    first.step()

    features = time_features(timesteps, w_time.shape[0])
    cond_act = jax.nn.silu(
        pooled + jnp.dot(features, w_time, preferred_element_type=jnp.float32)
    ).astype(jnp.bfloat16)
    mod_part = jnp.dot(cond_act, w_mod, preferred_element_type=jnp.float32).astype(jnp.bfloat16)
    modulation = lax.all_to_all(
        jnp.broadcast_to(mod_part[None], (tiles,) + mod_part.shape),
        "tile",
        split_axis=0,
        concat_axis=0,
        tiled=True,
    )
    modulation = jnp.moveaxis(modulation, 0, 1)
    modulation = modulation.reshape(group_count, 4, model_width)

    weights = head_weights(w_img, head_dim, heads_here)
    gains = jnp.stack(
        [
            jnp.tile(q_gain * query_factor, heads_here + spare),
            jnp.tile(k_gain, heads_here + spare),
        ]
    )
    group_of = jnp.arange(width) // head_dim
    sums = (group_of[:, None] == group_of[None, :]).astype(jnp.bfloat16)

    h_txt = modulate(text, modulation[:, None, 2], modulation[:, None, 3])
    qkv_txt = jnp.einsum("gtd,dc->gtc", h_txt, w_txt, preferred_element_type=jnp.float32).reshape(
        group_count, text_len, heads_here, 3, head_dim
    )
    text_qkv = jnp.concatenate(
        [
            rms_gain(qkv_txt[:, :, :, 0, :], text_q_gain * query_factor),
            rms_gain(qkv_txt[:, :, :, 1, :], text_k_gain),
            qkv_txt[:, :, :, 2, :].astype(jnp.bfloat16),
        ],
        axis=-1,
    )
    local_text = text_qkv
    if by_stride:
        local_text = text_to_send(text_qkv)
        text_qkv = text_to_strided(local_text, heads_here)
    text_qkv = jnp.pad(text_qkv, ((0, 0), (0, 0), (0, spare), (0, 0)))

    cover = min(512, seq_len)
    block = min(1024, seq_len)
    pairs = width // (2 * head_dim)
    lengths_of, mods, text_parts = [], [], []
    for slot in range(group_count):
        lengths_of.append(lax.dynamic_slice_in_dim(sorted_lengths, slot, 1))
        mod = lax.dynamic_index_in_dim(modulation, order[slot], 0, keepdims=False)
        mods.append(mod[0:2].astype(jnp.float32))
        one = lax.dynamic_index_in_dim(text_qkv, order[slot], 0, keepdims=False)
        text_parts.append(text_operands(one, head_dim, text_rows, text_keys))

    def project_step(slot, found, earlier):
        return project(
            lengths_of[slot],
            [source for _, source in found],
            [chunk for chunk, _ in found],
            mods[slot],
            [weights[i] for i in range(3)],
            gains,
            sums,
            seq_len,
            cover,
            head_dim,
            earlier,
        )

    def attend_text(slot, packed):
        query, key, value = text_parts[slot]
        operands = (lengths_of[slot], query, packed[1], packed[2], key, value)
        out = attend(*operands, 0, pairs, seq_len, text_rows, block, cover, False, True)
        return out[0:text_len, 0 : heads_here * head_dim]

    def attend_image(slot, packed, start, stop, many, shared, earlier=None):
        _, key, value = text_parts[slot]
        operands = (lengths_of[slot], *packed, key, value)
        return attend(
            *operands, start, stop, seq_len, many, block, cover, True, shared, earlier
        )

    def send_back(out):
        out = out[:, 0 : heads_here * head_dim].reshape(tiles, local_rows, -1)
        return lax.all_to_all(out, "tile", split_axis=0, concat_axis=0, tiled=True)

    image_attention = None
    image_back, text_outs = [], []
    spreading = first
    for slot in range(group_count):
        latest = slot == group_count - 1
        if slot > 0:
            following = Spread(after(tokens[slot], spreading.right, spreading.left))
            following.step()
            previous = project_step(slot - 1, spreading.found[-1], packed)
            outs = []
            for pair in range(pairs):
                earlier = outs[-1] if outs else None
                outs.append(
                    attend_image(slot - 1, previous, pair, pair + 1, block, True, earlier)
                )
            image_back.append([send_back(outs[-1])])
            text_outs.append(attend_text(slot - 1, after(previous, outs[-1])))
            following.join(outs[0])
            spreading = following
            for step in range(2, spreading.steps):
                spreading.step()
                if step == 2:
                    packed = project_step(slot, after(spreading.found[0], outs[-1]), None)
                else:
                    packed = project_step(slot, spreading.found[step - 2], packed)
                if step == spreading.steps - 1:
                    packed = project_step(slot, spreading.found[step - 1], packed)
                spreading.join(packed[0])
        else:
            spreading.join(mod_part)
            for step in range(2, spreading.steps):
                spreading.step()
                if step == 2:
                    packed = project_step(slot, spreading.found[0], None)
                packed = project_step(slot, spreading.found[step - 1], packed)
                spreading.join(*([packed[0], local_text] if step == 2 else [packed[0]]))
        if latest:
            packed = project_step(slot, spreading.found[-1], packed)
            parts = []
            for pair in range(pairs):
                out = attend_image(slot, packed, pair, pair + 1, block, False)
                parts.append(send_back(out))
            image_back.append(parts)
            text_outs.append(attend_text(slot, after(packed, out)))
            text_attention = jnp.stack(text_outs)[undo]
            if by_stride:
                text_attention = text_from_strided(text_attention, head_dim)

    if by_stride:
        for slot, parts in enumerate(image_back):
            place = lax.dynamic_slice_in_dim(order, slot, 1)
            image_attention = arrange(
                place, parts, image_attention, group_count, min(128, local_rows), head_dim
            )
    else:
        image_attention = jnp.stack(
            [
                jnp.concatenate(
                    [part.reshape(tiles, local_rows, -1, head_dim) for part in parts], axis=2
                )
                for parts in image_back
            ]
        )[undo]
        image_attention = jnp.transpose(image_attention, (0, 2, 1, 3, 4)).reshape(
            group_count, local_rows, tiles * heads_here * head_dim
        )
    return (image_attention, text_attention)


def solution(mesh):
    in_specs = (
        P("req", "tile", None),
        P("req", None, None),
        P("req", None),
        P("req"),
        P("req"),
        P(),
        P(None, "tile"),
        P(None, ("req", "tile")),
        P(None, "tile"),
        P(),
        P(),
        P(),
        P(),
    )
    out_specs = (P("req", "tile", None), P("req", None, "tile"))
    return jax.shard_map(local, mesh=mesh, in_specs=in_specs, out_specs=out_specs, check_vma=False)
```

```python
import functools, math
import jax, jax.numpy as jnp
from jax import lax
from jax.experimental import pallas as pl
from jax.experimental.pallas import tpu as pltpu
from jax.sharding import PartitionSpec as P

def attend_kernel(block, tail, masked, len_ref, q_ref, k_ref, v_ref, tk_ref, tv_ref, *refs):
    rows = pl.program_id(1)
    length = len_ref[0]
    out_ref = refs[-1]
    many = out_ref.shape[0]
    chunks = length // block
    rest = (length - chunks * block + tail - 1) // tail
    half = q_ref.shape[1] // 2

    def weigh(queries, keys, values):
        scores = jnp.dot(keys, queries, preferred_element_type=jnp.float32)
        return jnp.dot(
            values, jnp.exp2(scores).astype(jnp.bfloat16), preferred_element_type=jnp.float32
        )

    def run(queries):
        def body(size, first, c, carry):
            here = pl.ds(pl.multiple_of(first + c * size, size), size)
            return tuple(
                carry[h] + weigh(queries, k_ref[h, here, :], v_ref[h, :, here]) for h in range(2)
            )

        carry = tuple(weigh(queries, tk_ref[h], tv_ref[h]) for h in range(2))
        carry = lax.fori_loop(0, chunks, functools.partial(body, block, 0), carry)
        carry = lax.fori_loop(0, rest, functools.partial(body, tail, chunks * block), carry)
        out = jnp.concatenate([sums[0:half] / sums[half : half + 1] for sums in carry], axis=0)
        return jnp.transpose(out)

    if not masked:
        out_ref[...] = run(q_ref[0]).astype(jnp.bfloat16)
        return

    @pl.when(rows * many < length)
    def _():
        result = run(q_ref[0])
        spot = rows * many + lax.broadcasted_iota(jnp.int32, result.shape, 0)
        out_ref[...] = jnp.where(spot < length, result, 0.0).astype(jnp.bfloat16)

    @pl.when(rows * many >= length)
    def _():
        out_ref[...] = jnp.zeros_like(out_ref)


def attend(length, q, k, v, tk, tv, first, last, seq, many, block, tail, masked, shared, earlier=None):
    pairs, width, rows = q.shape
    rows = min(rows, seq)
    text_keys = tk.shape[1]
    into = first if shared else 0
    operands = [length, q, k, v, tk, tv]
    aliases = {}
    if earlier is not None:
        aliases = {len(operands): 0}
        operands.append(earlier)
    columns = (pairs if shared else last - first) * width

    def live(r, s):
        return jnp.minimum(r, (s[0] + many - 1) // many - 1) if masked else r

    return pl.pallas_call(
        functools.partial(attend_kernel, block, tail, masked),
        grid_spec=pltpu.PrefetchScalarGridSpec(
            num_scalar_prefetch=1,
            grid=(last - first, rows // many),
            in_specs=[
                pl.BlockSpec((1, width, many), lambda p, r, s: (p + first, 0, live(r, s))),
                pl.BlockSpec((2, seq, width), lambda p, r, s: (p + first, 0, 0)),
                pl.BlockSpec((2, width, seq), lambda p, r, s: (p + first, 0, 0)),
                pl.BlockSpec((2, text_keys, width), lambda p, r, s: (p + first, 0, 0)),
                pl.BlockSpec((2, width, text_keys), lambda p, r, s: (p + first, 0, 0)),
            ]
            + [pl.BlockSpec(memory_space=pl.ANY) for _ in aliases],
            out_specs=pl.BlockSpec((many, width), lambda p, r, s: (r, p + into)),
        ),
        out_shape=jax.ShapeDtypeStruct((rows, columns), jnp.bfloat16),
        input_output_aliases=aliases,
        compiler_params=pltpu.CompilerParams(
            dimension_semantics=("arbitrary", "arbitrary"), vmem_limit_bytes=48 << 20
        ),
        cost_estimate=pl.CostEstimate(flops=0, bytes_accessed=8 << 20, transcendentals=0),
        name="attend",
    )(*operands)


def arrange_kernel(head_dim, parts, order_ref, *refs):
    out_ref = refs[-1]
    width = 2 * head_dim
    tiles = refs[0].shape[0]
    start = 0
    for ref in refs[:parts]:
        for p in range(ref.shape[2] // width):
            for e in range(2):
                here = slice(p * width + e * head_dim, p * width + (e + 1) * head_dim)
                for a in range(tiles // 2):
                    both = [ref[2 * a, :, here], ref[2 * a + 1, :, here]]
                    out_ref[0, :, start : start + width] = jnp.concatenate(both, axis=1)
                    start += width


def arrange(place, parts, earlier, group_count, rows, head_dim):
    tiles, local_rows, _ = parts[0].shape
    operands = [place, *parts]
    aliases = {}
    if earlier is not None:
        aliases = {len(operands): 0}
        operands.append(earlier)
    total = sum(tiles * part.shape[2] for part in parts)
    return pl.pallas_call(
        functools.partial(arrange_kernel, head_dim, len(parts)),
        grid_spec=pltpu.PrefetchScalarGridSpec(
            num_scalar_prefetch=1,
            grid=(local_rows // rows,),
            in_specs=[
                pl.BlockSpec((tiles, rows, part.shape[2]), lambda r, s: (0, r, 0)) for part in parts
            ]
            + [pl.BlockSpec(memory_space=pl.ANY) for _ in aliases],
            out_specs=pl.BlockSpec((1, rows, total), lambda r, s: (s[0], r, 0)),
        ),
        out_shape=jax.ShapeDtypeStruct((group_count, local_rows, total), jnp.bfloat16),
        input_output_aliases=aliases,
        compiler_params=pltpu.CompilerParams(
            dimension_semantics=("arbitrary",), vmem_limit_bytes=48 << 20
        ),
        cost_estimate=pl.CostEstimate(
            flops=0, bytes_accessed=4 * local_rows * total, transcendentals=0
        ),
        name="arrange",
    )(*operands)


def project_kernel(head_dim, cover, chunks, spot_ref, *refs):
    x_refs = refs[:chunks]
    mod_ref, wq_ref, wk_ref, wv_ref, gain_ref, sum_ref = refs[chunks : chunks + 6]
    q_ref, k_ref, v_ref, x_buf, held, sems = refs[-6:]
    step = pl.program_id(0)
    rows, depth = held.shape
    length = spot_ref[chunks]
    start = spot_ref[step] * rows
    part = min(256, rows)
    group = 16

    def used(i):
        spot = spot_ref[i]
        return (spot >= 0) & (spot * rows < (length + cover - 1) // cover * cover)

    @pl.when(step == 0)
    def _():
        for i in range(chunks):

            @pl.when(used(i))
            def _():
                pltpu.make_async_copy(x_refs[i], x_buf.at[i], sems.at[i]).start()

    @pl.when(used(step))
    def _():
        pltpu.make_async_copy(x_refs[0], x_buf.at[step], sems.at[step]).wait()

        def normalize(base):
            for first in range(base, base + part, group):
                here = slice(first, first + group)
                x = x_buf[step, here, :].astype(jnp.float32)
                x = x - jnp.sum(x, axis=1, keepdims=True) * (1.0 / depth)
                spread = jnp.sum(x * x, axis=1, keepdims=True) * (1.0 / depth)
                h = x * lax.rsqrt(spread + epsilon)
                h = h * (1.0 + mod_ref[1:2, :]) + mod_ref[0:1, :]
                held[here, :] = h.astype(jnp.bfloat16)

        def norm(values, gain):
            squares = values * values
            high = squares.astype(jnp.bfloat16)
            low = (squares - high.astype(jnp.float32)).astype(jnp.bfloat16)
            total = jnp.dot(high, sum_ref[...], preferred_element_type=jnp.float32)
            total = total + jnp.dot(low, sum_ref[...], preferred_element_type=jnp.float32)
            return (values * lax.rsqrt(total * (1.0 / head_dim) + epsilon) * gain).astype(
                jnp.bfloat16
            )

        def product(base, w_ref):
            return jnp.dot(
                held[base : base + part, :], w_ref[...], preferred_element_type=jnp.float32
            )

        width = 2 * head_dim
        queries, keys, values = [], [], []
        normalize(0)
        for base in range(0, rows, part):
            if base + part < rows:
                normalize(base + part)
            query, key, value = [product(base, w) for w in (wq_ref, wk_ref, wv_ref)]
            queries.append(norm(query, gain_ref[0:1, :]))
            keys.append(norm(key, gain_ref[1:2, :]))
            values.append(value.astype(jnp.bfloat16))
        q, k, v = [jnp.concatenate(a, axis=0) for a in (queries, keys, values)]
        qt, vt = jnp.transpose(q), jnp.transpose(v)
        lane = lax.broadcasted_iota(jnp.int32, (rows, width), 1)
        live = start + lax.broadcasted_iota(jnp.int32, (head_dim, rows), 1) < length
        none = jnp.zeros((head_dim, rows), jnp.bfloat16)
        one = jnp.where(live, jnp.ones_like(none), none)
        gap = jnp.zeros((rows, width), jnp.bfloat16)
        for p in range(q.shape[1] // width):
            here = slice(p * width, (p + 1) * width)
            q_ref[p] = qt[here]
            k_ref[2 * p] = jnp.where(lane < head_dim, k[:, here], gap)
            k_ref[2 * p + 1] = jnp.where(lane < head_dim, gap, k[:, here])
            for h in (2 * p, 2 * p + 1):
                v_ref[h, 0:head_dim] = jnp.where(live, vt[h * head_dim : (h + 1) * head_dim], none)
                v_ref[h, head_dim:width] = one


def project(length, spots, tokens, mod, weights, gains, sums, seq, cover, head_dim, earlier):
    chunks = len(tokens)
    rows, depth = tokens[0].shape
    cols = weights[0].shape[1]
    heads = cols // head_dim
    width = 2 * head_dim
    blocks = seq // rows
    scalars = jnp.concatenate([jnp.stack(spots).astype(jnp.int32), length])

    def place(i, s):
        spot = s[i]
        used = (spot >= 0) & (spot * rows < (s[chunks] + cover - 1) // cover * cover)
        return jnp.where(used, spot, blocks)

    def whole(a):
        return pl.BlockSpec(a.shape, lambda i, s: (0,) * a.ndim)

    constants = [mod, *weights, gains, sums]
    operands = [scalars, *tokens, *constants]
    aliases = {}
    if earlier is not None:
        aliases = {len(operands) + i: i for i in range(3)}
        operands += list(earlier)
    padded = seq + max(rows, 128)
    return pl.pallas_call(
        functools.partial(project_kernel, head_dim, cover, chunks),
        grid_spec=pltpu.PrefetchScalarGridSpec(
            num_scalar_prefetch=1,
            grid=(chunks,),
            in_specs=[pl.BlockSpec(memory_space=pl.ANY) for _ in tokens]
            + [whole(a) for a in constants]
            + [pl.BlockSpec(memory_space=pl.ANY) for _ in aliases],
            out_specs=[
                pl.BlockSpec((heads // 2, width, rows), lambda i, s: (0, 0, place(i, s))),
                pl.BlockSpec((heads, rows, width), lambda i, s: (0, place(i, s), 0)),
                pl.BlockSpec((heads, width, rows), lambda i, s: (0, 0, place(i, s))),
            ],
            scratch_shapes=[
                pltpu.VMEM((chunks, rows, depth), jnp.bfloat16),
                pltpu.VMEM((rows, depth), jnp.bfloat16),
                pltpu.SemaphoreType.DMA((chunks,)),
            ],
        ),
        out_shape=[
            jax.ShapeDtypeStruct((heads // 2, width, padded), jnp.bfloat16),
            jax.ShapeDtypeStruct((heads, padded, width), jnp.bfloat16),
            jax.ShapeDtypeStruct((heads, width, padded), jnp.bfloat16),
        ],
        input_output_aliases=aliases,
        compiler_params=pltpu.CompilerParams(
            dimension_semantics=("arbitrary",), vmem_limit_bytes=48 << 20
        ),
        cost_estimate=pl.CostEstimate(flops=0, bytes_accessed=1 << 20, transcendentals=0),
        name="project",
    )(*operands)


epsilon = 1e-06


def time_features(step_index, feature_count):
    half_count = feature_count // 2
    frequency = jnp.exp(-math.log(10000.0) * jnp.arange(half_count, dtype=jnp.float32) / half_count)
    angles = step_index.astype(jnp.float32)[:, None] * frequency[None, :]
    return jnp.concatenate([jnp.cos(angles), jnp.sin(angles)], axis=-1).astype(jnp.bfloat16)


def modulate(tokens, shift, scale):
    values = tokens.astype(jnp.float32)
    center = jnp.mean(values, axis=-1, keepdims=True)
    spread = jnp.mean(jnp.square(values - center), axis=-1, keepdims=True)
    normed = (values - center) * lax.rsqrt(spread + epsilon)
    return (normed * (1.0 + scale.astype(jnp.float32)) + shift.astype(jnp.float32)).astype(
        jnp.bfloat16
    )


def rms_gain(vectors, gain):
    factor = lax.rsqrt(jnp.mean(jnp.square(vectors), axis=-1, keepdims=True) + epsilon)
    return (vectors * factor * gain).astype(jnp.bfloat16)


def head_weights(w_img, head_dim, heads_here):
    width = 3 * head_dim
    if strided(w_img, head_dim, heads_here):
        shards = lax.all_gather(w_img, "req", axis=0)
        depth = shards.shape[1]
        shards = shards.reshape(heads_here, depth, 3, head_dim)
    else:
        whole = lax.all_gather(w_img, ("req", "tile"), axis=1, tiled=True)
        depth = whole.shape[0]
        start = lax.axis_index("tile") * heads_here * width
        part = lax.dynamic_slice_in_dim(whole, start, heads_here * width, axis=1)
        shards = jnp.moveaxis(part.reshape(depth, heads_here, 3, head_dim), 1, 0)
    shards = jnp.pad(shards, ((0, heads_here % 2), (0, 0), (0, 0), (0, 0)))
    return jnp.transpose(shards, (2, 1, 0, 3)).reshape(3, depth, -1)


def strided(w_img, head_dim, heads_here):
    return (
        w_img.shape[1] == 3 * head_dim
        and heads_here == lax.axis_size("req")
        and lax.axis_size("tile") % heads_here == 0
    )


def text_to_send(qkv):
    tiles, mine, heads = lax.axis_size("tile"), lax.axis_index("tile"), qkv.shape[2]
    folds = tiles // heads
    parts = jnp.moveaxis(qkv, 2, 0)
    pick = (jnp.arange(folds) == mine % folds)[:, None, None, None, None]
    send = jnp.where(pick, parts[None], jnp.zeros_like(parts[None]))
    return lax.optimization_barrier(send.reshape((tiles,) + parts.shape[1:]))


def text_to_strided(send, heads):
    tiles, mine = lax.axis_size("tile"), lax.axis_index("tile")
    folds = tiles // heads
    got = lax.all_to_all(send, "tile", split_axis=0, concat_axis=0, tiled=True)
    got = got.reshape((heads, folds) + send.shape[1:])
    return jnp.moveaxis(
        lax.dynamic_index_in_dim(got, mine // heads, 1, keepdims=False), 0, 2
    )


def text_from_strided(out, head_dim):
    tiles, mine = lax.axis_size("tile"), lax.axis_index("tile")
    groups, text_len, width = out.shape
    heads = width // head_dim
    folds = tiles // heads
    parts = jnp.moveaxis(out.reshape(groups, text_len, heads, head_dim), 2, 0)
    got = lax.all_gather(parts, "tile", axis=0)
    got = got.reshape((folds, heads, heads) + parts.shape[1:])
    got = lax.dynamic_index_in_dim(got, mine % folds, 0, keepdims=False)
    got = lax.dynamic_index_in_dim(got, mine // folds, 1, keepdims=False)
    return jnp.moveaxis(got, 0, 2).reshape(groups, text_len, width)


def after(values, *others):
    return lax.optimization_barrier((values, others))[0]


class Spread:
    def __init__(self, tokens):
        self.tiles, self.mine = lax.axis_size("tile"), lax.axis_index("tile")
        self.pair = 2 if self.tiles % 2 == 0 else 1
        self.steps = self.tiles // self.pair
        self.right = self.left = tokens
        self.done = 0
        self.found = [self.both(tokens, self.mine)]

    def both(self, chunk, source):
        valid = (source >= 0) & (source < self.tiles)
        found = [(chunk, jnp.where(valid, source, -1))]
        if self.pair == 2:
            source = source + 1 - 2 * (self.mine % 2)
            swap = [(i, i ^ 1) for i in range(self.tiles)]
            found.append((lax.ppermute(chunk, "tile", swap), jnp.where(valid, source, -1)))
        return found

    def step(self):
        pairs = [(i, i + self.pair) for i in range(self.tiles - self.pair)]
        self.right = lax.ppermute(self.right, "tile", pairs)
        self.left = lax.ppermute(self.left, "tile", [(j, i) for i, j in pairs])
        self.done += 1

    def join(self, *others):
        self.right, self.left = after((self.right, self.left), *others)
        offset = self.pair * self.done
        self.found.append(
            self.both(self.right, self.mine - offset) + self.both(self.left, self.mine + offset)
        )


def text_operands(qkv, head_dim, rows, keys):
    text_len, heads = qkv.shape[0], qkv.shape[1]
    turned = jnp.transpose(qkv, (1, 2, 0))
    queries = turned[:, 0:head_dim].reshape(heads // 2, 2 * head_dim, text_len)
    queries = jnp.pad(queries, ((0, 0), (0, 0), (0, rows - text_len)))
    even = (jnp.arange(heads) % 2 == 0)[:, None, None]
    key = jnp.moveaxis(qkv[:, :, head_dim : 2 * head_dim], 1, 0)
    none = jnp.zeros_like(key)
    key = jnp.concatenate([jnp.where(even, key, none), jnp.where(even, none, key)], axis=2)
    key = jnp.pad(key, ((0, 0), (0, keys - text_len), (0, 0)))
    value = turned[:, 2 * head_dim : 3 * head_dim]
    value = jnp.concatenate([value, jnp.ones_like(value)], axis=1)
    value = jnp.pad(value, ((0, 0), (0, 0), (0, keys - text_len)))
    return queries, key, value


def local(
    image,
    text,
    pooled,
    timesteps,
    lengths,
    w_time,
    w_mod,
    w_img,
    w_txt,
    q_gain,
    k_gain,
    text_q_gain,
    text_k_gain,
):
    tiles = lax.axis_size("tile")
    group_count, local_rows, model_width = image.shape
    seq_len = local_rows * tiles
    text_len = text.shape[1]
    head_dim = q_gain.shape[0]
    heads_here = w_txt.shape[1] // (3 * head_dim)
    spare = heads_here % 2
    width = (heads_here + spare) * head_dim
    query_factor = head_dim ** (-0.5) * math.log2(math.e)
    text_rows = -(-text_len // 128) * 128
    text_keys = -(-text_len // 128) * 128
    by_stride = strided(w_img, head_dim, heads_here)

    if group_count == 2:
        longer = (lengths[1] > lengths[0]).astype(jnp.int32)
        order = undo = jnp.stack([longer, 1 - longer])
    else:
        order = jnp.argsort(-lengths)
        undo = jnp.argsort(order)
    sorted_lengths = lengths[order]
    tokens = [
        lax.dynamic_index_in_dim(image, order[slot], 0, keepdims=False)
        for slot in range(group_count)
    ]
    first = Spread(tokens[0])
    first.step()

    features = time_features(timesteps, w_time.shape[0])
    cond_act = jax.nn.silu(
        pooled + jnp.dot(features, w_time, preferred_element_type=jnp.float32)
    ).astype(jnp.bfloat16)
    mod_part = jnp.dot(cond_act, w_mod, preferred_element_type=jnp.float32).astype(jnp.bfloat16)
    modulation = lax.all_to_all(
        jnp.broadcast_to(mod_part[None], (tiles,) + mod_part.shape),
        "tile",
        split_axis=0,
        concat_axis=0,
        tiled=True,
    )
    modulation = jnp.moveaxis(modulation, 0, 1)
    modulation = modulation.reshape(group_count, 4, model_width)

    weights = head_weights(w_img, head_dim, heads_here)
    gains = jnp.stack(
        [
            jnp.tile(q_gain * query_factor, heads_here + spare),
            jnp.tile(k_gain, heads_here + spare),
        ]
    )
    group_of = jnp.arange(width) // head_dim
    sums = (group_of[:, None] == group_of[None, :]).astype(jnp.bfloat16)

    h_txt = modulate(text, modulation[:, None, 2], modulation[:, None, 3])
    qkv_txt = jnp.einsum("gtd,dc->gtc", h_txt, w_txt, preferred_element_type=jnp.float32).reshape(
        group_count, text_len, heads_here, 3, head_dim
    )
    text_qkv = jnp.concatenate(
        [
            rms_gain(qkv_txt[:, :, :, 0, :], text_q_gain * query_factor),
            rms_gain(qkv_txt[:, :, :, 1, :], text_k_gain),
            qkv_txt[:, :, :, 2, :].astype(jnp.bfloat16),
        ],
        axis=-1,
    )
    local_text = text_qkv
    if by_stride:
        local_text = text_to_send(text_qkv)
        text_qkv = text_to_strided(local_text, heads_here)
    text_qkv = jnp.pad(text_qkv, ((0, 0), (0, 0), (0, spare), (0, 0)))

    cover = min(512, seq_len)
    block = min(1024, seq_len)
    pairs = width // (2 * head_dim)
    lengths_of, mods, text_parts = [], [], []
    for slot in range(group_count):
        lengths_of.append(lax.dynamic_slice_in_dim(sorted_lengths, slot, 1))
        mod = lax.dynamic_index_in_dim(modulation, order[slot], 0, keepdims=False)
        mods.append(mod[0:2].astype(jnp.float32))

    def prepare_text(slot, text_qkv):
        one = lax.dynamic_index_in_dim(text_qkv, order[slot], 0, keepdims=False)
        text_parts.append(text_operands(one, head_dim, text_rows, text_keys))

    def project_step(slot, found, earlier):
        return project(
            lengths_of[slot],
            [source for _, source in found],
            [chunk for chunk, _ in found],
            mods[slot],
            [weights[i] for i in range(3)],
            gains,
            sums,
            seq_len,
            cover,
            head_dim,
            earlier,
        )

    def attend_text(slot, packed):
        query, key, value = text_parts[slot]
        operands = (lengths_of[slot], query, packed[1], packed[2], key, value)
        out = attend(*operands, 0, pairs, seq_len, text_rows, block, cover, False, True)
        return out[0:text_len, 0 : heads_here * head_dim]

    def attend_image(slot, packed, start, stop, many, shared, earlier=None):
        _, key, value = text_parts[slot]
        operands = (lengths_of[slot], *packed, key, value)
        return attend(
            *operands, start, stop, seq_len, many, block, cover, True, shared, earlier
        )

    def send_back(out):
        out = out[:, 0 : heads_here * head_dim].reshape(tiles, local_rows, -1)
        return lax.all_to_all(out, "tile", split_axis=0, concat_axis=0, tiled=True)

    image_attention = None
    image_back, text_outs = [], []
    spreading = first
    for slot in range(group_count):
        latest = slot == group_count - 1
        if slot > 0:
            following = Spread(after(tokens[slot], spreading.right, spreading.left))
            following.step()
            previous = project_step(slot - 1, spreading.found[-1], packed)
            text_qkv = after(text_qkv, previous[0])
            prepare_text(slot - 1, text_qkv)
            outs = []
            for pair in range(pairs):
                earlier = outs[-1] if outs else None
                outs.append(
                    attend_image(slot - 1, previous, pair, pair + 1, block, True, earlier)
                )
            image_back.append([send_back(outs[-1])])
            text_outs.append(attend_text(slot - 1, after(previous, outs[-1])))
            following.join(outs[0])
            spreading = following
            for step in range(2, spreading.steps):
                spreading.step()
                if step == 2:
                    packed = project_step(slot, after(spreading.found[0], outs[-1]), None)
                else:
                    packed = after(packed, text_outs[-1])
                    packed = project_step(slot, spreading.found[step - 2], packed)
                if step == spreading.steps - 1:
                    packed = project_step(slot, spreading.found[step - 1], packed)
                spreading.join(packed[0])
        else:
            spreading.join(mod_part)
            for step in range(2, spreading.steps):
                spreading.step()
                if step == 2:
                    packed = project_step(slot, spreading.found[0], None)
                packed = project_step(slot, spreading.found[step - 1], packed)
                spreading.join(*([packed[0], local_text] if step == 2 else [packed[0]]))
        if latest:
            packed = project_step(slot, spreading.found[-1], packed)
            prepare_text(slot, text_qkv)
            parts = []
            for pair in range(pairs):
                out = attend_image(slot, packed, pair, pair + 1, block, False)
                parts.append(send_back(out))
                packed = after(packed, out)
                if pair == 0:
                    text_outs.append(attend_text(slot, packed))
                    packed = after(packed, text_outs[-1])
            image_back.append(parts)
            text_attention = jnp.stack(text_outs)[undo]
            if by_stride:
                text_attention = text_from_strided(text_attention, head_dim)

    if by_stride:
        for slot, parts in enumerate(image_back):
            place = lax.dynamic_slice_in_dim(order, slot, 1)
            image_attention = arrange(
                place, parts, image_attention, group_count, min(128, local_rows), head_dim
            )
    else:
        image_attention = jnp.stack(
            [
                jnp.concatenate(
                    [part.reshape(tiles, local_rows, -1, head_dim) for part in parts], axis=2
                )
                for parts in image_back
            ]
        )[undo]
        image_attention = jnp.transpose(image_attention, (0, 2, 1, 3, 4)).reshape(
            group_count, local_rows, tiles * heads_here * head_dim
        )
    return (image_attention, text_attention)


def solution(mesh):
    in_specs = (
        P("req", "tile", None),
        P("req", None, None),
        P("req", None),
        P("req"),
        P("req"),
        P(),
        P(None, "tile"),
        P(None, ("req", "tile")),
        P(None, "tile"),
        P(),
        P(),
        P(),
        P(),
    )
    out_specs = (P("req", "tile", None), P("req", None, "tile"))
    return jax.shard_map(local, mesh=mesh, in_specs=in_specs, out_specs=out_specs, check_vma=False)
```

```python
import functools, math
import jax, jax.numpy as jnp
from jax import lax
from jax.experimental import pallas as pl
from jax.experimental.pallas import tpu as pltpu
from jax.sharding import PartitionSpec as P

def attend_kernel(block, tail, masked, len_ref, q_ref, k_ref, v_ref, tk_ref, tv_ref, *refs):
    rows = pl.program_id(1)
    length = len_ref[0]
    out_ref = refs[-1]
    many = out_ref.shape[0]
    chunks = length // block
    rest = (length - chunks * block + tail - 1) // tail
    half = q_ref.shape[1] // 2

    def weigh(queries, keys, values):
        scores = jnp.dot(keys, queries, preferred_element_type=jnp.float32)
        return jnp.dot(
            values, jnp.exp2(scores).astype(jnp.bfloat16), preferred_element_type=jnp.float32
        )

    def run(queries):
        def body(size, first, c, carry):
            here = pl.ds(pl.multiple_of(first + c * size, size), size)
            return tuple(
                carry[h] + weigh(queries, k_ref[h, here, :], v_ref[h, :, here]) for h in range(2)
            )

        carry = tuple(weigh(queries, tk_ref[h], tv_ref[h]) for h in range(2))
        carry = lax.fori_loop(0, chunks, functools.partial(body, block, 0), carry)
        carry = lax.fori_loop(0, rest, functools.partial(body, tail, chunks * block), carry)
        out = jnp.concatenate([sums[0:half] / sums[half : half + 1] for sums in carry], axis=0)
        return jnp.transpose(out)

    if not masked:
        out_ref[...] = run(q_ref[0]).astype(jnp.bfloat16)
        return

    @pl.when(rows * many < length)
    def _():
        result = run(q_ref[0])
        spot = rows * many + lax.broadcasted_iota(jnp.int32, result.shape, 0)
        out_ref[...] = jnp.where(spot < length, result, 0.0).astype(jnp.bfloat16)

    @pl.when(rows * many >= length)
    def _():
        out_ref[...] = jnp.zeros_like(out_ref)


def attend(length, q, k, v, tk, tv, first, last, seq, many, block, tail, masked, shared, earlier=None):
    pairs, width, rows = q.shape
    rows = min(rows, seq)
    text_keys = tk.shape[1]
    into = first if shared else 0
    operands = [length, q, k, v, tk, tv]
    aliases = {}
    if earlier is not None:
        aliases = {len(operands): 0}
        operands.append(earlier)
    columns = (pairs if shared else last - first) * width

    def live(r, s):
        return jnp.minimum(r, (s[0] + many - 1) // many - 1) if masked else r

    return pl.pallas_call(
        functools.partial(attend_kernel, block, tail, masked),
        grid_spec=pltpu.PrefetchScalarGridSpec(
            num_scalar_prefetch=1,
            grid=(last - first, rows // many),
            in_specs=[
                pl.BlockSpec((1, width, many), lambda p, r, s: (p + first, 0, live(r, s))),
                pl.BlockSpec((2, seq, width), lambda p, r, s: (p + first, 0, 0)),
                pl.BlockSpec((2, width, seq), lambda p, r, s: (p + first, 0, 0)),
                pl.BlockSpec((2, text_keys, width), lambda p, r, s: (p + first, 0, 0)),
                pl.BlockSpec((2, width, text_keys), lambda p, r, s: (p + first, 0, 0)),
            ]
            + [pl.BlockSpec(memory_space=pl.ANY) for _ in aliases],
            out_specs=pl.BlockSpec((many, width), lambda p, r, s: (r, p + into)),
        ),
        out_shape=jax.ShapeDtypeStruct((rows, columns), jnp.bfloat16),
        input_output_aliases=aliases,
        compiler_params=pltpu.CompilerParams(
            dimension_semantics=("arbitrary", "arbitrary"), vmem_limit_bytes=48 << 20
        ),
        cost_estimate=pl.CostEstimate(flops=0, bytes_accessed=8 << 20, transcendentals=0),
        name="attend",
    )(*operands)


def arrange_kernel(head_dim, parts, order_ref, *refs):
    out_ref = refs[-1]
    width = 2 * head_dim
    tiles = refs[0].shape[0]
    start = 0
    for ref in refs[:parts]:
        for p in range(ref.shape[2] // width):
            for e in range(2):
                here = slice(p * width + e * head_dim, p * width + (e + 1) * head_dim)
                for a in range(tiles // 2):
                    both = [ref[2 * a, :, here], ref[2 * a + 1, :, here]]
                    out_ref[0, :, start : start + width] = jnp.concatenate(both, axis=1)
                    start += width


def arrange(place, parts, earlier, group_count, rows, head_dim):
    tiles, local_rows, _ = parts[0].shape
    operands = [place, *parts]
    aliases = {}
    if earlier is not None:
        aliases = {len(operands): 0}
        operands.append(earlier)
    total = sum(tiles * part.shape[2] for part in parts)
    return pl.pallas_call(
        functools.partial(arrange_kernel, head_dim, len(parts)),
        grid_spec=pltpu.PrefetchScalarGridSpec(
            num_scalar_prefetch=1,
            grid=(local_rows // rows,),
            in_specs=[
                pl.BlockSpec((tiles, rows, part.shape[2]), lambda r, s: (0, r, 0)) for part in parts
            ]
            + [pl.BlockSpec(memory_space=pl.ANY) for _ in aliases],
            out_specs=pl.BlockSpec((1, rows, total), lambda r, s: (s[0], r, 0)),
        ),
        out_shape=jax.ShapeDtypeStruct((group_count, local_rows, total), jnp.bfloat16),
        input_output_aliases=aliases,
        compiler_params=pltpu.CompilerParams(
            dimension_semantics=("arbitrary",), vmem_limit_bytes=48 << 20
        ),
        cost_estimate=pl.CostEstimate(
            flops=0, bytes_accessed=4 * local_rows * total, transcendentals=0
        ),
        name="arrange",
    )(*operands)


def project_kernel(head_dim, cover, chunks, spot_ref, *refs):
    x_refs = refs[:chunks]
    mod_ref, wq_ref, wk_ref, wv_ref, gain_ref, sum_ref = refs[chunks : chunks + 6]
    q_ref, k_ref, v_ref, x_buf, held, sems = refs[-6:]
    step = pl.program_id(0)
    rows, depth = held.shape
    length = spot_ref[chunks]
    start = spot_ref[step] * rows
    part = min(256, rows)
    group = 16

    def used(i):
        spot = spot_ref[i]
        return (spot >= 0) & (spot * rows < (length + cover - 1) // cover * cover)

    @pl.when(step == 0)
    def _():
        for i in range(chunks):

            @pl.when(used(i))
            def _():
                pltpu.make_async_copy(x_refs[i], x_buf.at[i], sems.at[i]).start()

    @pl.when(used(step))
    def _():
        pltpu.make_async_copy(x_refs[0], x_buf.at[step], sems.at[step]).wait()

        def normalize(base):
            for first in range(base, base + part, group):
                here = slice(first, first + group)
                x = x_buf[step, here, :].astype(jnp.float32)
                x = x - jnp.sum(x, axis=1, keepdims=True) * (1.0 / depth)
                spread = jnp.sum(x * x, axis=1, keepdims=True) * (1.0 / depth)
                h = x * lax.rsqrt(spread + epsilon)
                h = h * (1.0 + mod_ref[1:2, :]) + mod_ref[0:1, :]
                held[here, :] = h.astype(jnp.bfloat16)

        def norm(values, gain):
            squares = values * values
            high = squares.astype(jnp.bfloat16)
            low = (squares - high.astype(jnp.float32)).astype(jnp.bfloat16)
            total = jnp.dot(high, sum_ref[...], preferred_element_type=jnp.float32)
            total = total + jnp.dot(low, sum_ref[...], preferred_element_type=jnp.float32)
            return (values * lax.rsqrt(total * (1.0 / head_dim) + epsilon) * gain).astype(
                jnp.bfloat16
            )

        def product(base, w_ref):
            return jnp.dot(
                held[base : base + part, :], w_ref[...], preferred_element_type=jnp.float32
            )

        width = 2 * head_dim
        queries, keys, values = [], [], []
        normalize(0)
        for base in range(0, rows, part):
            if base + part < rows:
                normalize(base + part)
            query, key, value = [product(base, w) for w in (wq_ref, wk_ref, wv_ref)]
            queries.append(norm(query, gain_ref[0:1, :]))
            keys.append(norm(key, gain_ref[1:2, :]))
            values.append(value.astype(jnp.bfloat16))
        q, k, v = [jnp.concatenate(a, axis=0) for a in (queries, keys, values)]
        qt, vt = jnp.transpose(q), jnp.transpose(v)
        lane = lax.broadcasted_iota(jnp.int32, (rows, width), 1)
        live = start + lax.broadcasted_iota(jnp.int32, (head_dim, rows), 1) < length
        none = jnp.zeros((head_dim, rows), jnp.bfloat16)
        one = jnp.where(live, jnp.ones_like(none), none)
        gap = jnp.zeros((rows, width), jnp.bfloat16)
        for p in range(q.shape[1] // width):
            here = slice(p * width, (p + 1) * width)
            q_ref[p] = qt[here]
            k_ref[2 * p] = jnp.where(lane < head_dim, k[:, here], gap)
            k_ref[2 * p + 1] = jnp.where(lane < head_dim, gap, k[:, here])
            for h in (2 * p, 2 * p + 1):
                v_ref[h, 0:head_dim] = jnp.where(live, vt[h * head_dim : (h + 1) * head_dim], none)
                v_ref[h, head_dim:width] = one


def project(length, spots, tokens, mod, weights, gains, sums, seq, cover, head_dim, earlier):
    chunks = len(tokens)
    rows, depth = tokens[0].shape
    cols = weights[0].shape[1]
    heads = cols // head_dim
    width = 2 * head_dim
    blocks = seq // rows
    scalars = jnp.concatenate([jnp.stack(spots).astype(jnp.int32), length])

    def place(i, s):
        spot = s[i]
        used = (spot >= 0) & (spot * rows < (s[chunks] + cover - 1) // cover * cover)
        return jnp.where(used, spot, blocks)

    def whole(a):
        return pl.BlockSpec(a.shape, lambda i, s: (0,) * a.ndim)

    constants = [mod, *weights, gains, sums]
    operands = [scalars, *tokens, *constants]
    aliases = {}
    if earlier is not None:
        aliases = {len(operands) + i: i for i in range(3)}
        operands += list(earlier)
    padded = seq + max(rows, 128)
    return pl.pallas_call(
        functools.partial(project_kernel, head_dim, cover, chunks),
        grid_spec=pltpu.PrefetchScalarGridSpec(
            num_scalar_prefetch=1,
            grid=(chunks,),
            in_specs=[pl.BlockSpec(memory_space=pl.ANY) for _ in tokens]
            + [whole(a) for a in constants]
            + [pl.BlockSpec(memory_space=pl.ANY) for _ in aliases],
            out_specs=[
                pl.BlockSpec((heads // 2, width, rows), lambda i, s: (0, 0, place(i, s))),
                pl.BlockSpec((heads, rows, width), lambda i, s: (0, place(i, s), 0)),
                pl.BlockSpec((heads, width, rows), lambda i, s: (0, 0, place(i, s))),
            ],
            scratch_shapes=[
                pltpu.VMEM((chunks, rows, depth), jnp.bfloat16),
                pltpu.VMEM((rows, depth), jnp.bfloat16),
                pltpu.SemaphoreType.DMA((chunks,)),
            ],
        ),
        out_shape=[
            jax.ShapeDtypeStruct((heads // 2, width, padded), jnp.bfloat16),
            jax.ShapeDtypeStruct((heads, padded, width), jnp.bfloat16),
            jax.ShapeDtypeStruct((heads, width, padded), jnp.bfloat16),
        ],
        input_output_aliases=aliases,
        compiler_params=pltpu.CompilerParams(
            dimension_semantics=("arbitrary",), vmem_limit_bytes=48 << 20
        ),
        cost_estimate=pl.CostEstimate(flops=0, bytes_accessed=1 << 20, transcendentals=0),
        name="project",
    )(*operands)


epsilon = 1e-06


def time_features(step_index, feature_count):
    half_count = feature_count // 2
    frequency = jnp.exp(-math.log(10000.0) * jnp.arange(half_count, dtype=jnp.float32) / half_count)
    angles = step_index.astype(jnp.float32)[:, None] * frequency[None, :]
    return jnp.concatenate([jnp.cos(angles), jnp.sin(angles)], axis=-1).astype(jnp.bfloat16)


def modulate(tokens, shift, scale):
    values = tokens.astype(jnp.float32)
    center = jnp.mean(values, axis=-1, keepdims=True)
    spread = jnp.mean(jnp.square(values - center), axis=-1, keepdims=True)
    normed = (values - center) * lax.rsqrt(spread + epsilon)
    return (normed * (1.0 + scale.astype(jnp.float32)) + shift.astype(jnp.float32)).astype(
        jnp.bfloat16
    )


def rms_gain(vectors, gain):
    factor = lax.rsqrt(jnp.mean(jnp.square(vectors), axis=-1, keepdims=True) + epsilon)
    return (vectors * factor * gain).astype(jnp.bfloat16)


def head_weights(w_img, head_dim, heads_here):
    width = 3 * head_dim
    if strided(w_img, head_dim, heads_here):
        shards = lax.all_gather(w_img, "req", axis=0)
        depth = shards.shape[1]
        shards = shards.reshape(heads_here, depth, 3, head_dim)
    else:
        whole = lax.all_gather(w_img, ("req", "tile"), axis=1, tiled=True)
        depth = whole.shape[0]
        start = lax.axis_index("tile") * heads_here * width
        part = lax.dynamic_slice_in_dim(whole, start, heads_here * width, axis=1)
        shards = jnp.moveaxis(part.reshape(depth, heads_here, 3, head_dim), 1, 0)
    shards = jnp.pad(shards, ((0, heads_here % 2), (0, 0), (0, 0), (0, 0)))
    return jnp.transpose(shards, (2, 1, 0, 3)).reshape(3, depth, -1)


def strided(w_img, head_dim, heads_here):
    return (
        w_img.shape[1] == 3 * head_dim
        and heads_here == lax.axis_size("req")
        and lax.axis_size("tile") % heads_here == 0
    )


def text_to_send(qkv):
    tiles, mine, heads = lax.axis_size("tile"), lax.axis_index("tile"), qkv.shape[2]
    folds = tiles // heads
    parts = jnp.moveaxis(qkv, 2, 0)
    pick = (jnp.arange(folds) == mine % folds)[:, None, None, None, None]
    send = jnp.where(pick, parts[None], jnp.zeros_like(parts[None]))
    return lax.optimization_barrier(send.reshape((tiles,) + parts.shape[1:]))


def text_to_strided(send, heads):
    tiles, mine = lax.axis_size("tile"), lax.axis_index("tile")
    folds = tiles // heads
    got = lax.all_to_all(send, "tile", split_axis=0, concat_axis=0, tiled=True)
    got = got.reshape((heads, folds) + send.shape[1:])
    return jnp.moveaxis(
        lax.dynamic_index_in_dim(got, mine // heads, 1, keepdims=False), 0, 2
    )


def text_from_strided(out, head_dim):
    tiles, mine = lax.axis_size("tile"), lax.axis_index("tile")
    groups, text_len, width = out.shape
    heads = width // head_dim
    folds = tiles // heads
    parts = jnp.moveaxis(out.reshape(groups, text_len, heads, head_dim), 2, 0)
    got = lax.all_gather(parts, "tile", axis=0)
    got = got.reshape((folds, heads, heads) + parts.shape[1:])
    got = lax.dynamic_index_in_dim(got, mine % folds, 0, keepdims=False)
    got = lax.dynamic_index_in_dim(got, mine // folds, 1, keepdims=False)
    return jnp.moveaxis(got, 0, 2).reshape(groups, text_len, width)


def after(values, *others):
    return lax.optimization_barrier((values, others))[0]


class Spread:
    def __init__(self, tokens):
        self.tiles, self.mine = lax.axis_size("tile"), lax.axis_index("tile")
        self.pair = 2 if self.tiles % 2 == 0 else 1
        self.steps = self.tiles // self.pair
        self.right = self.left = tokens
        self.done = 0
        self.found = [self.both(tokens, self.mine)]

    def both(self, chunk, source):
        valid = (source >= 0) & (source < self.tiles)
        found = [(chunk, jnp.where(valid, source, -1))]
        if self.pair == 2:
            source = source + 1 - 2 * (self.mine % 2)
            swap = [(i, i ^ 1) for i in range(self.tiles)]
            found.append((lax.ppermute(chunk, "tile", swap), jnp.where(valid, source, -1)))
        return found

    def step(self):
        pairs = [(i, i + self.pair) for i in range(self.tiles - self.pair)]
        self.right = lax.ppermute(self.right, "tile", pairs)
        self.left = lax.ppermute(self.left, "tile", [(j, i) for i, j in pairs])
        self.done += 1

    def join(self, *others):
        self.right, self.left = after((self.right, self.left), *others)
        offset = self.pair * self.done
        self.found.append(
            self.both(self.right, self.mine - offset) + self.both(self.left, self.mine + offset)
        )


def text_operands(qkv, head_dim, rows, keys):
    text_len, heads = qkv.shape[0], qkv.shape[1]
    turned = jnp.transpose(qkv, (1, 2, 0))
    queries = turned[:, 0:head_dim].reshape(heads // 2, 2 * head_dim, text_len)
    queries = jnp.pad(queries, ((0, 0), (0, 0), (0, rows - text_len)))
    even = (jnp.arange(heads) % 2 == 0)[:, None, None]
    key = jnp.moveaxis(qkv[:, :, head_dim : 2 * head_dim], 1, 0)
    none = jnp.zeros_like(key)
    key = jnp.concatenate([jnp.where(even, key, none), jnp.where(even, none, key)], axis=2)
    key = jnp.pad(key, ((0, 0), (0, keys - text_len), (0, 0)))
    value = turned[:, 2 * head_dim : 3 * head_dim]
    value = jnp.concatenate([value, jnp.ones_like(value)], axis=1)
    value = jnp.pad(value, ((0, 0), (0, 0), (0, keys - text_len)))
    return queries, key, value


def local(
    image,
    text,
    pooled,
    timesteps,
    lengths,
    w_time,
    w_mod,
    w_img,
    w_txt,
    q_gain,
    k_gain,
    text_q_gain,
    text_k_gain,
):
    tiles = lax.axis_size("tile")
    group_count, local_rows, model_width = image.shape
    seq_len = local_rows * tiles
    text_len = text.shape[1]
    head_dim = q_gain.shape[0]
    heads_here = w_txt.shape[1] // (3 * head_dim)
    spare = heads_here % 2
    width = (heads_here + spare) * head_dim
    query_factor = head_dim ** (-0.5) * math.log2(math.e)
    text_rows = -(-text_len // 128) * 128
    text_keys = -(-text_len // 128) * 128
    by_stride = strided(w_img, head_dim, heads_here)

    if group_count == 2:
        longer = (lengths[1] > lengths[0]).astype(jnp.int32)
        order = undo = jnp.stack([longer, 1 - longer])
    else:
        order = jnp.argsort(-lengths)
        undo = jnp.argsort(order)
    sorted_lengths = lengths[order]
    tokens = [
        lax.dynamic_index_in_dim(image, order[slot], 0, keepdims=False)
        for slot in range(group_count)
    ]
    first = Spread(tokens[0])
    first.step()

    features = time_features(timesteps, w_time.shape[0])
    cond_act = jax.nn.silu(
        pooled + jnp.dot(features, w_time, preferred_element_type=jnp.float32)
    ).astype(jnp.bfloat16)
    mod_part = jnp.dot(cond_act, w_mod, preferred_element_type=jnp.float32).astype(jnp.bfloat16)
    modulation = lax.all_to_all(
        jnp.broadcast_to(mod_part[None], (tiles,) + mod_part.shape),
        "tile",
        split_axis=0,
        concat_axis=0,
        tiled=True,
    )
    modulation = jnp.moveaxis(modulation, 0, 1)
    modulation = modulation.reshape(group_count, 4, model_width)

    weights = head_weights(w_img, head_dim, heads_here)
    gains = jnp.stack(
        [
            jnp.tile(q_gain * query_factor, heads_here + spare),
            jnp.tile(k_gain, heads_here + spare),
        ]
    )
    group_of = jnp.arange(width) // head_dim
    sums = (group_of[:, None] == group_of[None, :]).astype(jnp.bfloat16)

    h_txt = modulate(text, modulation[:, None, 2], modulation[:, None, 3])
    qkv_txt = jnp.einsum("gtd,dc->gtc", h_txt, w_txt, preferred_element_type=jnp.float32).reshape(
        group_count, text_len, heads_here, 3, head_dim
    )
    text_qkv = jnp.concatenate(
        [
            rms_gain(qkv_txt[:, :, :, 0, :], text_q_gain * query_factor),
            rms_gain(qkv_txt[:, :, :, 1, :], text_k_gain),
            qkv_txt[:, :, :, 2, :].astype(jnp.bfloat16),
        ],
        axis=-1,
    )
    local_text = text_qkv
    if by_stride:
        local_text = text_to_send(text_qkv)
        text_qkv = text_to_strided(local_text, heads_here)
    text_qkv = jnp.pad(text_qkv, ((0, 0), (0, 0), (0, spare), (0, 0)))

    cover = min(512, seq_len)
    block = min(1024, seq_len)
    pairs = width // (2 * head_dim)
    lengths_of, mods, text_parts = [], [], []
    for slot in range(group_count):
        lengths_of.append(lax.dynamic_slice_in_dim(sorted_lengths, slot, 1))
        mod = lax.dynamic_index_in_dim(modulation, order[slot], 0, keepdims=False)
        mods.append(mod[0:2].astype(jnp.float32))
        one = lax.dynamic_index_in_dim(text_qkv, order[slot], 0, keepdims=False)
        text_parts.append(text_operands(one, head_dim, text_rows, text_keys))

    def project_step(slot, found, earlier):
        return project(
            lengths_of[slot],
            [source for _, source in found],
            [chunk for chunk, _ in found],
            mods[slot],
            [weights[i] for i in range(3)],
            gains,
            sums,
            seq_len,
            cover,
            head_dim,
            earlier,
        )

    def attend_text(slot, packed):
        query, key, value = text_parts[slot]
        operands = (lengths_of[slot], query, packed[1], packed[2], key, value)
        out = attend(*operands, 0, pairs, seq_len, text_rows, block, cover, False, True)
        return out[0:text_len, 0 : heads_here * head_dim]

    def attend_image(slot, packed, start, stop, many, shared, earlier=None):
        _, key, value = text_parts[slot]
        operands = (lengths_of[slot], *packed, key, value)
        return attend(
            *operands, start, stop, seq_len, many, block, cover, True, shared, earlier
        )

    def send_back(out):
        out = out[:, 0 : heads_here * head_dim].reshape(tiles, local_rows, -1)
        return lax.all_to_all(out, "tile", split_axis=0, concat_axis=0, tiled=True)

    image_attention = None
    image_back, text_outs = [], []
    spreading = first
    for slot in range(group_count):
        latest = slot == group_count - 1
        if slot > 0:
            following = Spread(after(tokens[slot], spreading.right, spreading.left))
            following.step()
            previous = project_step(slot - 1, spreading.found[-1], packed)
            outs = []
            for pair in range(pairs):
                earlier = outs[-1] if outs else None
                outs.append(
                    attend_image(slot - 1, previous, pair, pair + 1, block, True, earlier)
                )
            image_back.append([send_back(outs[-1])])
            text_outs.append(attend_text(slot - 1, after(previous, outs[-1])))
            following.join(outs[0])
            spreading = following
            for step in range(2, spreading.steps):
                spreading.step()
                if step == 2:
                    packed = project_step(slot, after(spreading.found[0], outs[-1]), None)
                else:
                    found = after(spreading.found[step - 2], text_outs[-1])
                    packed = project_step(slot, found, packed)
                if step == spreading.steps - 1:
                    packed = project_step(slot, spreading.found[step - 1], packed)
                spreading.join(packed[0])
        else:
            spreading.join(mod_part)
            for step in range(2, spreading.steps):
                spreading.step()
                if step == 2:
                    packed = project_step(slot, spreading.found[0], None)
                packed = project_step(slot, spreading.found[step - 1], packed)
                spreading.join(*([packed[0], local_text] if step == 2 else [packed[0]]))
        if latest:
            packed = project_step(slot, spreading.found[-1], packed)
            parts = []
            for pair in range(pairs):
                out = attend_image(slot, packed, pair, pair + 1, block, False)
                parts.append(send_back(out))
            image_back.append(parts)
            text_outs.append(attend_text(slot, after(packed, out)))
            text_attention = jnp.stack(text_outs)[undo]
            if by_stride:
                text_attention = text_from_strided(text_attention, head_dim)

    if by_stride:
        for slot, parts in enumerate(image_back):
            place = lax.dynamic_slice_in_dim(order, slot, 1)
            image_attention = arrange(
                place, parts, image_attention, group_count, min(128, local_rows), head_dim
            )
    else:
        image_attention = jnp.stack(
            [
                jnp.concatenate(
                    [part.reshape(tiles, local_rows, -1, head_dim) for part in parts], axis=2
                )
                for parts in image_back
            ]
        )[undo]
        image_attention = jnp.transpose(image_attention, (0, 2, 1, 3, 4)).reshape(
            group_count, local_rows, tiles * heads_here * head_dim
        )
    return (image_attention, text_attention)


def solution(mesh):
    in_specs = (
        P("req", "tile", None),
        P("req", None, None),
        P("req", None),
        P("req"),
        P("req"),
        P(),
        P(None, "tile"),
        P(None, ("req", "tile")),
        P(None, "tile"),
        P(),
        P(),
        P(),
        P(),
    )
    out_specs = (P("req", "tile", None), P("req", None, "tile"))
    return jax.shard_map(local, mesh=mesh, in_specs=in_specs, out_specs=out_specs, check_vma=False)
```
